256 devices in a mesh: own: 64 (over x, z, core), grp: 4 (over y).
Axes of the slice: x: 4, y: 4, z: 8, core: 2. Of those that a mesh axis runs over, the one named last changes fastest.
Arguments:
- amplitudes: bfloat16 [38912, 5632], P(('own', 'grp'))
- integrals: bfloat16 [196608, 512], P('own'), may hold values from -6 to 6
- task_owner: int32 [2816, 1], replicated, may hold values from 0 to 63; in each aligned block of 44 rows (0 to 43, 44 to 87, ...) at most 2 rows name the same one
- task_slot: int32 [2816, 1], replicated, may hold values from 0 to 23
- occ_pair: float32 [38912], P(('own', 'grp')), may hold values from -4 to -1
- vir_pair: float32 [512], replicated, may hold values from 0.5 to 4
Outputs:
- update: float32 [38912, 512], P(('own', 'grp'))
- root_mean: float32 [], replicated
The draws below stay inside these ranges and needn't reach their ends.
Inputs may be any that keep to these rules, and one draw needn't show every extreme that they name: `task_owner`: in each aligned block of 44 rows (one owner's list) at most 2 rows name the same owner, and some block has exactly 2.
All inputs are finite; a program needn't handle non-finite values.
Results may differ from the reference program's by a relative error of at most 0.0003.
Values may be sent and summed in bfloat16 or wider, within the bound.
A program may use at most 128 MiB of HBM per device.

```python
import math
import jax
import jax.numpy as jnp
import numpy as np
from jax import lax

TILE = 128
AB_WINDOW = 512
CD_DEV = 24
NEED = 44
MOST = 2
ROWS = 38912
NCD = 1536
TASKS = 2816
N_OWN = 64


def draw_amplitudes(key, part):
    key = jax.random.fold_in(key, 11)
    col_key, base_key = jax.random.split(key, 2)
    columns = NEED * TILE
    row_frac = jnp.arange(ROWS, dtype=jnp.float32) / ROWS
    row_scale = jnp.exp(math.log(10.0) * row_frac)
    col_scale = jnp.exp(math.log(10.0) * jax.random.uniform(col_key, (columns,), jnp.float32))
    base_draw = jax.random.normal(base_key, (ROWS, columns), jnp.float32)
    factor = 1.0 / (4.64 * math.sqrt(columns))
    return (base_draw * row_scale[:, None] * col_scale[None, :] * factor).astype(jnp.bfloat16)


def plant(array, own_key, least, top_value):
    place = [jax.random.randint(jax.random.fold_in(own_key, axis), (), 0, length) for axis, length in enumerate(array.shape)]
    widest = array.shape.index(max(array.shape))
    next_to = place[:widest] + [(place[widest] + 1) % array.shape[widest]] + place[widest + 1:]
    return array.at[tuple(place)].set(least).at[tuple(next_to)].set(top_value)


def shard_levels(own_key, dims, cuts, low, top_value):
    factor_of = 1.0
    for position, shards_of in cuts:
        draws = jax.random.uniform(jax.random.fold_in(jax.random.fold_in(own_key, 6), position), (shards_of,), jnp.float32, low / len(cuts), top_value / len(cuts))
        factor_of = factor_of * jnp.repeat(jnp.exp(draws), dims[position] // shards_of).reshape((-1,) + (1,) * (len(dims) - 1 - position))
    return factor_of


def shared_out(key, own, number, rows, amount, top, reach, slope):
    order = jax.random.permutation(key, amount)
    heavy_load, ordinary = load_shares(amount, rows * top, reach, slope, True), load_shares(amount, rows * top, reach, slope, False)
    places = jnp.arange(amount)

    def named(sizes, rotation):
        used = int((sizes > 0).sum())
        fixed = max(1, used // 4)
        moved = fixed + (places - fixed + rotation * (used - fixed)) % max(1, amount - fixed)
        return jnp.zeros((amount,), jnp.int32).at[order[jnp.where(places < fixed, places, moved)]].set(jnp.asarray(sizes, jnp.int32))

    sizes = jnp.where(number % 4 == 0, named(heavy_load, number // 4), named(ordinary, number - number // 4 - 1))
    mixed = jax.random.permutation(jax.random.fold_in(own, 3), amount)
    source_of, taker = mixed[0:amount // 2 * 2:2], mixed[1:amount // 2 * 2:2]
    margin = jnp.minimum(sizes[source_of] - 1, reach - sizes[taker]) // 2
    margin = jnp.where((source_of == order[0]) | (taker == order[0]) | (sizes[taker] == 0), 0, jnp.maximum(margin, 0))
    moved = jax.random.randint(jax.random.fold_in(own, 4), (amount // 2,), 0, 1 << 20) % (margin + 1)
    sizes = sizes.at[source_of].add(-moved).at[taker].add(moved)
    items = jnp.searchsorted(jnp.cumsum(sizes), jnp.arange(rows * top), side="right").astype(jnp.int32)
    table = items.reshape(top, rows).T
    table = table[jax.random.permutation(jax.random.fold_in(own, 1), rows)]
    rotation = jax.random.randint(jax.random.fold_in(own, 2), (rows, 1), 0, top)
    return jnp.take_along_axis(table, (jnp.arange(top)[None, :] + rotation) % top, axis=1)


def load_shares(number_of, total, bound, lean, full):
    weights = [(1 << 20) // math.isqrt(grade ** lean) + 1 for grade in range(1, number_of + 1)]
    largest = bound if full else min(bound, max(-(-total // number_of), total * weights[0] // sum(weights)))
    least = 1 if total - largest >= number_of - 1 else 0
    holding, rest = [largest] + [least] * (number_of - 1), total - largest - least * (number_of - 1)
    while rest > 0:
        free = [i for i in range(1, number_of) if holding[i] < largest] or [i for i in range(1, number_of) if holding[i] < bound]
        mass, left = sum([weights[i] for i in free]), rest
        for i in free:
            more = min(bound - holding[i], max(1, left * weights[i] // mass), rest)
            holding[i] = holding[i] + more
            rest = rest - more
    return np.array(holding)


def noise(stream_key, dims, width, limit, shards=(), held_as=jnp.bfloat16):
    loudness = shard_levels(stream_key, dims, shards, -0.22, 0.18) if shards else 1.0
    drawn = jax.random.normal(stream_key, dims, jnp.float32) * width * loudness
    return jnp.minimum(jnp.maximum(drawn, -limit), limit).astype(held_as)


def setup_inputs(seed: int = 0) -> dict:
    key_list = jax.random.split(jax.random.key(seed), 7)
    amplitudes = draw_amplitudes(jax.random.fold_in(key_list[6], 71), 0)
    integrals = noise(key_list[1], (NCD * TILE, AB_WINDOW), 1.0, 6.0, ((0, 64),))
    task_owner_keys = jax.random.split(jax.random.fold_in(key_list[2], 1), TASKS // NEED)
    task_owner_turns = jax.random.permutation(jax.random.fold_in(key_list[2], 3), TASKS // NEED)
    task_owner = jax.vmap(lambda own, number: shared_out(jax.random.fold_in(key_list[2], 2), own, number, NEED, N_OWN, 1, MOST, 2))(task_owner_keys, task_owner_turns).reshape((TASKS, 1))
    task_slot = plant(jax.random.randint(key_list[3], (TASKS, 1), 0, CD_DEV), jax.random.fold_in(key_list[3], 1), 0, CD_DEV - 1).astype(jnp.int32)
    occ_pair = jnp.clip(-4.0 + 3.0 * jax.random.uniform(key_list[4], (ROWS,), jnp.float32) ** shard_levels(key_list[4], (ROWS,), ((0, 256),), -0.2, 0.2), -4.0, -1.0)
    vir_pair = jnp.clip(jax.random.uniform(key_list[5], (AB_WINDOW,), jnp.float32, 0.5, 4.0), 0.5, 4.0)
    return dict(amplitudes=amplitudes, integrals=integrals, task_owner=task_owner, task_slot=task_slot, occ_pair=occ_pair, vir_pair=vir_pair)


def reference(amplitudes, integrals, task_owner, task_slot, occ_pair, vir_pair):
    tile_stack = integrals.reshape(NCD, TILE, AB_WINDOW)
    tile_ids = (task_owner[:, 0] * CD_DEV + task_slot[:, 0]).astype(jnp.int32).reshape(N_OWN, NEED)
    row_blocks = amplitudes.reshape(N_OWN, ROWS // N_OWN, NEED * TILE)
    occ_blocks = occ_pair.reshape(N_OWN, ROWS // N_OWN)

    def per_owner(inputs):
        block_rows, owner_ids, occ_rows = inputs
        selected = jnp.take(tile_stack, owner_ids, axis=0).reshape(NEED * TILE, AB_WINDOW)
        product = jnp.dot(block_rows, selected, preferred_element_type=jnp.float32)
        return product / (occ_rows[:, None] - vir_pair[None, :])
    update = lax.map(per_owner, (row_blocks, tile_ids, occ_blocks)).reshape(ROWS, AB_WINDOW)
    root_mean = jnp.sqrt(jnp.sum(update * update) / (ROWS * AB_WINDOW))
    return (update, root_mean)
```

```python
import jax
import jax.numpy as jnp
from jax import lax
from jax.experimental import pallas as pl
from jax.experimental.pallas import tpu as pltpu
from jax.sharding import PartitionSpec as P

MESH = pl.DeviceIdType.MESH
TILE = 128
CD_DEV = 24
NEED = 44
OWNERS = 64
NX, NY, NZ = 4, 4, 8
LANES = 128
PIECES = 4
PIECE = CD_DEV // PIECES
SHIFTS = (0, -1, 1, -2, 2)
TASKS_AT = len(SHIFTS) * OWNERS * 2


def kernel(
    rows, total_entries, tab, integ, amp, occ, vir, out, rms,
    g0, gm1, gp1, gm2, gp2, got, sx, sd, a0, am, ap, ao, stack, mine, cols, occs,
    sum1, sum2, sum3, load_sem, z_send, z_recv, y_send, y_recv, x_send, d_send, got_recv,
    occ_send, occ_recv, u_send, u_recv, s_send, s1_recv, s2_recv, s3_recv,
):
    own, y = lax.axis_index("own"), lax.axis_index("grp")
    x, z, c = lax.div(own, 16), lax.rem(lax.div(own, 2), 8), lax.rem(own, 2)
    half = amp.shape[1] // 2

    def at(dx=0, dy=0, dz=0, dc=0):
        nx, nz = lax.rem(x + dx + NX, NX), lax.rem(z + dz + NZ, NZ)
        return (nx * 16 + nz * 2 + lax.rem(c + dc, 2), lax.rem(y + dy + NY, NY))

    def line(dx=0, dc=0):
        return lax.rem(x + dx + NX, NX) * 2 + lax.rem(c + dc, 2)

    def send(src, dst, send_sem, recv_sem, device):
        copy = pltpu.make_async_remote_copy(
            src_ref=src, dst_ref=dst, send_sem=send_sem, recv_sem=recv_sem,
            device_id=device, device_id_type=MESH,
        )
        copy.start()
        started.append(copy)

    def arrived(dst, recv_sem):
        pltpu.make_async_remote_copy(
            src_ref=dst, dst_ref=dst, send_sem=recv_sem, recv_sem=recv_sem,
            device_id=at(0, 0, 1, 0), device_id_type=MESH,
        ).wait_recv()

    started = []
    near = [(m // 2, m % 2) for m in range(1, 8)]
    every = [(m // 2, m % 2) for m in range(8)]

    loads = []
    for p in range(PIECES):
        loads.append(pltpu.make_async_copy(
            integ.at[pl.ds(p * PIECE, PIECE), :, pl.ds(pl.multiple_of(y * LANES, LANES), LANES)],
            g0.at[pl.ds(p * PIECE, PIECE)], load_sem.at[p]))
    loads.append(pltpu.make_async_copy(amp, a0, load_sem.at[PIECES]))
    for copy in loads:
        copy.start()

    targets = [(dx, 0, 0, dc) for dx, dc in near]
    targets += [(dx, 0, dz, dc) for dz in (1, -1) for dx, dc in every]
    targets += [(dx, 0, 2, 0) for dx in range(NX)] + [(dx, 0, -2, 1) for dx in range(NX)]
    targets += [(0, dy, 0, 0) for dy in (1, 2, 3)]
    targets += [(0, 0, dz, 0) for dz in (-2, 3, -3, 4)]
    barrier = pltpu.get_barrier_semaphore()
    for dx, dy, dz, dc in targets:
        pl.semaphore_signal(barrier, inc=1, device_id=at(-dx, -dy, -dz, dc), device_id_type=MESH)
    occs[0] = jnp.broadcast_to(occ[...], occs.shape[1:])
    pl.semaphore_wait(barrier, len(targets))

    right, left = at(0, 0, 1, 0), at(0, 0, -1, 0)
    for p in range(PIECES):
        loads[p].wait()
        part = pl.ds(p * PIECE, PIECE)
        send(g0.at[part], gm1.at[part], z_send.at[0, 0, p], z_recv.at[0, 0, p], right)
        send(g0.at[part], gp1.at[part], z_send.at[1, 0, p], z_recv.at[1, 0, p], left)
    loads[PIECES].wait()
    low, high = pl.ds(0, half), pl.ds(half, half)
    up, down = at(0, 1, 0, 0), at(0, -1, 0, 0)
    send(a0.at[:, low], am.at[:, low], y_send.at[0], y_recv.at[0], up)
    send(a0.at[:, high], ap.at[:, high], y_send.at[1], y_recv.at[1], down)
    send(a0.at[:, high], am.at[:, high], y_send.at[2], y_recv.at[2], up)
    send(a0.at[:, low], ap.at[:, low], y_send.at[3], y_recv.at[3], down)
    for dy in (1, 2, 3):
        send(occs.at[0], occs.at[NY - dy], occ_send.at[dy], occ_recv.at[NY - dy], at(0, dy, 0, 0))

    def pick(block, k, r, reader):
        return block[tab[(k * OWNERS + reader) * 2 + r]]

    def across(k, block):
        phase = SHIFTS[k] % NZ
        place = pl.ds(phase * 16 + line() * 2, 2)
        for i, (dx, dc) in enumerate(near):
            device = at(dx, 0, 0, dc)
            for r in range(2):
                sx[k, i, r] = pick(block, k, r, device[0])
            send(sx.at[k, i], got.at[place], x_send.at[k, i], got_recv.at[phase, line()], device)
        for r in range(2):
            got[phase * 16 + line() * 2 + r] = pick(block, k, r, own)

    def far(k, block, slot, dz, dx, dc):
        phase = (SHIFTS[k] - dz) % NZ
        place = pl.ds(phase * 16 + line() * 2, 2)
        device = at(dx, 0, dz, dc)
        for r in range(2):
            sd[slot, r] = pick(block, k, r, device[0])
        send(sd.at[slot], got.at[place], d_send.at[slot], got_recv.at[phase, line()], device)

    across(0, g0)
    for p in range(PIECES):
        part = pl.ds(p * PIECE, PIECE)
        arrived(gm1.at[part], z_recv.at[0, 0, p])
        send(gm1.at[part], gm2.at[part], z_send.at[0, 1, p], z_recv.at[0, 1, p], right)
        arrived(gp1.at[part], z_recv.at[1, 0, p])
        send(gp1.at[part], gp2.at[part], z_send.at[1, 1, p], z_recv.at[1, 1, p], left)
    across(1, gm1)
    across(2, gp1)
    arrived(am.at[:, low], y_recv.at[0])
    send(am.at[:, low], ao.at[:, low], y_send.at[4], y_recv.at[4], up)
    arrived(ap.at[:, high], y_recv.at[1])
    send(ap.at[:, high], ao.at[:, high], y_send.at[5], y_recv.at[5], down)

    for p in range(PIECES):
        arrived(gm2.at[pl.ds(p * PIECE, PIECE)], z_recv.at[0, 1, p])
    for dx in range(NX):
        far(3, gm2, dx, 2, dx, 0)
    for i, (dx, dc) in enumerate(every):
        far(3, gm2, 4 + i, 1, dx, dc)
    for p in range(PIECES):
        arrived(gp2.at[pl.ds(p * PIECE, PIECE)], z_recv.at[1, 1, p])
    for dx in range(NX):
        far(4, gp2, 12 + dx, -2, dx, 1)
    for i, (dx, dc) in enumerate(every):
        far(4, gp2, 16 + i, -1, dx, dc)
    across(3, gm2)
    across(4, gp2)

    arrived(am.at[:, high], y_recv.at[2])
    arrived(ap.at[:, low], y_recv.at[3])
    for dy in (1, 2, 3):
        arrived(occs.at[dy], occ_recv.at[dy])
    arrived(ao.at[:, low], y_recv.at[4])
    arrived(ao.at[:, high], y_recv.at[5])
    for phase in (0, 7, 1, 6, 2, 5, 3, 4):
        for dx, dc in (every if phase in (3, 4, 5) else near):
            other = line(dx, dc)
            arrived(got.at[pl.ds(phase * 16 + other * 2, 2)], got_recv.at[phase, other])

    for t in range(NEED):
        stack[pl.ds(t * TILE, TILE)] = got[tab[TASKS_AT + t]]
    square = jnp.zeros((8, LANES), jnp.float32)
    diagonal = lax.broadcasted_iota(jnp.int32, (rows, rows), 0) == lax.broadcasted_iota(jnp.int32, (rows, rows), 1)
    for dy, block in enumerate((a0, ap, ao, am)):
        ladder = jnp.dot(block[...], stack[...], preferred_element_type=jnp.float32)
        occ_rows = jnp.sum(jnp.where(diagonal, occs[dy, 0:1, :], 0.0), axis=1, keepdims=True)
        update = ladder / (occ_rows - vir[y])
        square = square + jnp.sum((update * update).reshape(rows // 8, 8, LANES), axis=0)
        if dy == 0:
            cols[y] = update
        else:
            mine[dy] = update
            send(mine.at[dy], cols.at[y], u_send.at[dy], u_recv.at[y], at(0, dy, 0, 0))

    sum1[line()] = square
    for i, (dx, dc) in enumerate(near):
        send(sum1.at[line()], sum1.at[line()], s_send.at[i], s1_recv.at[line()], at(dx, 0, 0, dc))
    for dx, dc in near:
        arrived(sum1.at[line(dx, dc)], s1_recv.at[line(dx, dc)])
    sum2[y] = jnp.sum(sum1[...], axis=0)
    for dy in (1, 2, 3):
        send(sum2.at[y], sum2.at[y], s_send.at[6 + dy], s2_recv.at[y], at(0, dy, 0, 0))
    for dy in (1, 2, 3):
        other = lax.rem(y + dy, NY)
        arrived(sum2.at[other], s2_recv.at[other])
    sum3[z] = jnp.sum(sum2[...], axis=0)
    for dz in range(1, NZ):
        send(sum3.at[z], sum3.at[z], s_send.at[9 + dz], s3_recv.at[z], at(0, 0, dz, 0))
    for dy in (1, 2, 3):
        other = lax.rem(y + dy, NY)
        arrived(cols.at[other], u_recv.at[other])
    for k in range(NY):
        out[:, k * LANES:(k + 1) * LANES] = cols[k]
    for dz in range(1, NZ):
        other = lax.rem(z + dz, NZ)
        arrived(sum3.at[other], s3_recv.at[other])
    whole = jnp.sum(jnp.sum(sum3[...], axis=0), axis=(0, 1), keepdims=True)
    rms[...] = jnp.broadcast_to(jnp.sqrt(whole / total_entries), rms.shape)
    for copy in started:
        copy.wait_send()


def tables(task_owner, task_slot):
    own = lax.axis_index("own")
    line, z = own - (lax.rem(lax.div(own, 2), 8)) * 2, lax.rem(lax.div(own, 2), 8)
    owners = task_owner.reshape(OWNERS, NEED)
    slots = task_slot.reshape(OWNERS, NEED)
    shifts = jnp.array(SHIFTS, jnp.int32)
    sources = line + lax.rem(z + shifts + NZ, NZ) * 2
    same = owners[None] == sources[:, None, None]
    first = jnp.min(jnp.where(same, slots[None], CD_DEV - 1), axis=2)
    last = jnp.max(jnp.where(same, slots[None], 0), axis=2)
    sends = jnp.stack([first, last], axis=2).reshape(-1)
    my_owners = lax.dynamic_index_in_dim(owners, own, 0, keepdims=False)
    my_slots = lax.dynamic_index_in_dim(slots, own, 0, keepdims=False)
    mates = my_owners[None, :] == my_owners[:, None]
    least = jnp.min(jnp.where(mates, my_slots[None, :], CD_DEV), axis=1)
    rank = (my_slots > least).astype(jnp.int32)
    zs = lax.rem(lax.div(my_owners, 2), 8)
    xs, cs = lax.div(my_owners, 16), lax.rem(my_owners, 2)
    takes = lax.rem(zs - z + NZ, NZ) * 16 + (xs * 2 + cs) * 2 + rank
    return jnp.concatenate([sends, takes])


def per_device(amplitudes, integrals, task_owner, task_slot, occ_pair, vir_pair):
    rows, depth = amplitudes.shape
    columns = integrals.shape[1]
    tab = tables(task_owner, task_slot)
    bf16, f32 = jnp.bfloat16, jnp.float32
    dma = pltpu.SemaphoreType.DMA
    tile = (CD_DEV, TILE, LANES)

    def body(*refs):
        kernel(rows, float(rows * OWNERS * NY * columns), *refs)

    update, rms = pl.pallas_call(
        body,
        out_shape=(
            jax.ShapeDtypeStruct((rows, columns), f32),
            jax.ShapeDtypeStruct((8, LANES), f32),
        ),
        in_specs=[
            pl.BlockSpec(memory_space=pltpu.SMEM),
            pl.BlockSpec(memory_space=pl.ANY),
            pl.BlockSpec(memory_space=pl.ANY),
            pl.BlockSpec(memory_space=pltpu.VMEM),
            pl.BlockSpec(memory_space=pltpu.VMEM),
        ],
        out_specs=(
            pl.BlockSpec(memory_space=pltpu.VMEM),
            pl.BlockSpec(memory_space=pltpu.VMEM),
        ),
        scratch_shapes=[
            *[pltpu.VMEM(tile, bf16)] * 5,
            pltpu.VMEM((2 * OWNERS, TILE, LANES), bf16),
            pltpu.VMEM((5, 7, 2, TILE, LANES), bf16),
            pltpu.VMEM((24, 2, TILE, LANES), bf16),
            *[pltpu.VMEM((rows, depth), bf16)] * 4,
            pltpu.VMEM((depth, LANES), bf16),
            pltpu.VMEM((NY, rows, LANES), f32),
            pltpu.VMEM((NY, rows, LANES), f32),
            pltpu.VMEM((NY, 8, rows), f32),
            pltpu.VMEM((8, 8, LANES), f32),
            pltpu.VMEM((NY, 8, LANES), f32),
            pltpu.VMEM((NZ, 8, LANES), f32),
            dma((PIECES + 1,)),
            dma((2, 2, PIECES)), dma((2, 2, PIECES)),
            dma((6,)), dma((6,)),
            dma((5, 7)), dma((24,)), dma((NZ, 8)),
            dma((NY,)), dma((NY,)),
            dma((NY,)), dma((NY,)),
            dma((17,)), dma((8,)), dma((NY,)), dma((NZ,)),
        ],
        compiler_params=pltpu.CompilerParams(
            collective_id=0, has_side_effects=True, vmem_limit_bytes=48 << 20
        ),
        cost_estimate=pl.CostEstimate(
            flops=2 * rows * depth * columns, bytes_accessed=8 << 20, transcendentals=0
        ),
        name="ladder",
    )(
        tab,
        integrals.reshape(CD_DEV, TILE, columns),
        amplitudes,
        occ_pair.reshape(1, rows),
        vir_pair.reshape(NY, 1, LANES),
    )
    return update, rms[0, 0]


def solution(mesh):
    placed = (P(("own", "grp"), None), P("own", None), P(), P(), P(("own", "grp")), P())
    return jax.shard_map(
        per_device,
        mesh=mesh,
        in_specs=placed,
        out_specs=(P(("own", "grp"), None), P()),
        check_vma=False,
    )
```

```python
import jax
import jax.numpy as jnp
from jax import lax
from jax.experimental import pallas as pl
from jax.experimental.pallas import tpu as pltpu
from jax.sharding import PartitionSpec as P

MESH = pl.DeviceIdType.MESH
TILE = 128
PART = 64
PARTS = 2
CD_DEV = 24
NEED = 44
OWNERS = 64
NX, NY, NZ = 4, 4, 8
LANES = 128
SHIFTS = (0, -1, 1, -2, 2)
NEAR = [(m // 2, m % 2) for m in range(1, 8)]
EVERY = [(m // 2, m % 2) for m in range(8)]


def fill_tables(own, x, z, c, owner_row, slot_row, owners, slots, table, takes):
    for reader in range(OWNERS):
        listed = slice(reader * NEED, (reader + 1) * NEED)
        owners[reader:reader + 1, :] = owner_row[0:1, listed]
        slots[reader:reader + 1, :] = slot_row[0:1, listed]
    lane = lax.broadcasted_iota(jnp.int32, (OWNERS, LANES), 1)
    filled = jnp.zeros((OWNERS, LANES), jnp.int32)
    for k, shift in enumerate(SHIFTS):
        source = x * 16 + lax.rem(z + shift + NZ, NZ) * 2 + c
        same = owners[...] == source
        first = jnp.min(jnp.where(same, slots[...], CD_DEV - 1), axis=1, keepdims=True)
        last = jnp.max(jnp.where(same, slots[...], 0), axis=1, keepdims=True)
        filled = jnp.where(lane == 2 * k, first, filled)
        filled = jnp.where(lane == 2 * k + 1, last, filled)
    table[...] = filled
    mine, wanted = owners[pl.ds(own, 1), :], slots[pl.ds(own, 1), :]
    square = (NEED, NEED)
    diagonal = lax.broadcasted_iota(jnp.int32, square, 0) == lax.broadcasted_iota(jnp.int32, square, 1)
    down_mine = jnp.sum(jnp.where(diagonal, mine, 0), axis=1, keepdims=True)
    down_wanted = jnp.sum(jnp.where(diagonal, wanted, 0), axis=1, keepdims=True)
    least = jnp.min(jnp.where(down_mine == mine, down_wanted, CD_DEV), axis=0, keepdims=True)
    second = (wanted > least).astype(jnp.int32)
    at_z = lax.shift_right_logical(mine, 1) & 7
    at_line = lax.shift_right_logical(mine, 4) * 2 + (mine & 1)
    place = ((at_z - z + NZ) & 7) * 16 + at_line * 2 + second
    takes[...] = jnp.zeros(takes.shape, jnp.int32)
    takes[:, 0:NEED] = jnp.broadcast_to(place, (8, NEED))


def kernel(
    rows, total_entries, owner_list, slot_list, integ, amp, occ, vir, out, rms,
    owner_row, slot_row, owners, slots, table, takes, tab, own_tab, g0a, g0b, gm1a, gm1b, gp1a, gp1b, gm2a, gm2b, gp2a, gp2b, gota, gotb,
    sx, sd, a0, am, ap, ao, stack, mine, cols, occs, virs,
    sum1, sum2, load_sem, z_send, z_recv, y_send, y_recv, x_send, d_send, got_recv,
    occ_send, occ_recv, u_send, u_recv, s_send, s1_recv, s2_recv,
):
    g0, gm1, gp1, gm2, gp2, got = (g0a, g0b), (gm1a, gm1b), (gp1a, gp1b), (gm2a, gm2b), (gp2a, gp2b), (gota, gotb)
    own, y = lax.axis_index("own"), lax.axis_index("grp")
    x, z, c = lax.div(own, 16), lax.rem(lax.div(own, 2), 8), lax.rem(own, 2)
    half = amp.shape[1] // 2

    def at(dx=0, dy=0, dz=0, dc=0):
        nx, nz = lax.rem(x + dx + NX, NX), lax.rem(z + dz + NZ, NZ)
        return (nx * 16 + nz * 2 + lax.rem(c + dc, 2), lax.rem(y + dy + NY, NY))

    def line(dx=0, dc=0):
        return lax.rem(x + dx + NX, NX) * 2 + lax.rem(c + dc, 2)

    started = []

    def send(src, dst, send_sem, recv_sem, device, later=True):
        copy = pltpu.make_async_remote_copy(
            src_ref=src, dst_ref=dst, send_sem=send_sem, recv_sem=recv_sem,
            device_id=device, device_id_type=MESH,
        )
        copy.start()
        if later:
            started.append(copy)
        return copy

    def arrived(dst, recv_sem):
        pltpu.make_async_remote_copy(
            src_ref=dst, dst_ref=dst, send_sem=recv_sem, recv_sem=recv_sem,
            device_id=at(0, 0, 1, 0), device_id_type=MESH,
        ).wait_recv()

    barrier = pltpu.get_barrier_semaphore()
    targets = [(0, 0, 1, 0), (0, 0, -1, 0)] + [(dx, 0, 0, dc) for dx, dc in NEAR] + [(0, dy, 0, 0) for dy in (1, 2, 3)]
    for dx, dy, dz, dc in targets:
        pl.semaphore_signal(barrier, inc=1, device_id=at(-dx, -dy, -dz, dc), device_id_type=MESH)
    loads = []
    for h in range(PARTS):
        loads.append(pltpu.make_async_copy(
            integ.at[:, pl.ds(h * PART, PART), pl.ds(pl.multiple_of(y * LANES, LANES), LANES)],
            g0[h], load_sem.at[h]))
    loads.append(pltpu.make_async_copy(amp, a0, load_sem.at[2]))
    loads.append(pltpu.make_async_copy(occ, occs.at[0], load_sem.at[3]))
    loads.append(pltpu.make_async_copy(vir, virs, load_sem.at[4]))
    loads.append(pltpu.make_async_copy(owner_list, owner_row, load_sem.at[5]))
    loads.append(pltpu.make_async_copy(slot_list, slot_row, load_sem.at[6]))
    for copy in loads:
        copy.start()
    loads[0].wait()
    pl.semaphore_wait(barrier, len(targets))

    right, left = at(0, 0, 1, 0), at(0, 0, -1, 0)
    low, high = pl.ds(0, half), pl.ds(half, half)
    up, down = at(0, 1, 0, 0), at(0, -1, 0, 0)

    def pick(block, k, r, reader):
        return block[tab[reader, 2 * k + r]]

    def across(k, h, block):
        phase = SHIFTS[k] % NZ
        place = pl.ds(phase * 16 + line() * 2, 2)
        for i, (dx, dc) in enumerate(NEAR):
            device = at(dx, 0, 0, dc)
            for r in range(2):
                sx[h, k, i, r] = pick(block, k, r, device[0])
            send(sx.at[h, k, i], got[h].at[place], x_send.at[h, k, i], got_recv.at[h, phase, line()], device)
        for r in range(2):
            got[h][phase * 16 + line() * 2 + r] = pick(block, k, r, own)

    def far(k, h, block, slot, dz, dx, dc):
        phase = (SHIFTS[k] - dz) % NZ
        place = pl.ds(phase * 16 + line() * 2, 2)
        device = at(dx, 0, dz, dc)
        for r in range(2):
            sd[h, slot, r] = pick(block, k, r, device[0])
        send(sd.at[h, slot], got[h].at[place], d_send.at[h, slot], got_recv.at[h, phase, line()], device)

    def first_hop(h, later=True):
        return (
            send(g0[h], gm1[h], z_send.at[0, 0, h], z_recv.at[0, 0, h], right, later),
            send(g0[h], gp1[h], z_send.at[1, 0, h], z_recv.at[1, 0, h], left, later),
        )

    def second_hop(h):
        arrived(gm1[h], z_recv.at[0, 0, h])
        send(gm1[h], gm2[h], z_send.at[0, 1, h], z_recv.at[0, 1, h], right)
        arrived(gp1[h], z_recv.at[1, 0, h])
        send(gp1[h], gp2[h], z_send.at[1, 1, h], z_recv.at[1, 1, h], left)

    def last_hops(h):
        arrived(gm2[h], z_recv.at[0, 1, h])
        arrived(gp2[h], z_recv.at[1, 1, h])
        for dx in range(NX):
            far(3, h, gm2[h], dx, 2, dx, 0)
            far(4, h, gp2[h], 12 + dx, -2, dx, 1)
        for i, (dx, dc) in enumerate(EVERY):
            far(3, h, gm2[h], 4 + i, 1, dx, dc)
            far(4, h, gp2[h], 16 + i, -1, dx, dc)
        across(3, h, gm2[h])
        across(4, h, gp2[h])

    first = first_hop(0, False)
    for copy in loads[1:]:
        copy.wait()
    first_rows = (
        send(a0.at[:, low], am.at[:, low], y_send.at[0], y_recv.at[0], up, False),
        send(a0.at[:, high], ap.at[:, high], y_send.at[1], y_recv.at[1], down, False),
    )
    for dy in (1, 2, 3):
        send(occs.at[0], occs.at[NY - dy], occ_send.at[dy], occ_recv.at[NY - dy], at(0, dy, 0, 0))
    fill_tables(own, x, z, c, owner_row, slot_row, owners, slots, table, takes)
    to_scalar = (pltpu.make_async_copy(table, tab, load_sem.at[7]), pltpu.make_async_copy(takes, own_tab, load_sem.at[8]))
    for copy in to_scalar:
        copy.start()
    for copy in to_scalar:
        copy.wait()
    across(0, 0, g0[0])
    for copy in first:
        copy.wait_send()
    first_hop(1)
    across(0, 1, g0[1])
    second_hop(0)
    across(1, 0, gm1[0])
    across(2, 0, gp1[0])
    for copy in first_rows:
        copy.wait_send()
    send(a0.at[:, high], am.at[:, high], y_send.at[2], y_recv.at[2], up)
    send(a0.at[:, low], ap.at[:, low], y_send.at[3], y_recv.at[3], down)
    second_hop(1)
    arrived(am.at[:, low], y_recv.at[0])
    send(am.at[:, low], ao.at[:, low], y_send.at[4], y_recv.at[4], up)
    arrived(ap.at[:, high], y_recv.at[1])
    send(ap.at[:, high], ao.at[:, high], y_send.at[5], y_recv.at[5], down)
    across(1, 1, gm1[1])
    across(2, 1, gp1[1])
    last_hops(0)
    last_hops(1)

    for dy in (1, 2, 3):
        arrived(occs.at[dy], occ_recv.at[dy])
    for h in range(PARTS):
        for phase in (0, 7, 1, 6, 2, 5, 3, 4):
            for dx, dc in (EVERY if phase in (3, 4, 5) else NEAR):
                other = line(dx, dc)
                arrived(got[h].at[pl.ds(phase * 16 + other * 2, 2)], got_recv.at[h, phase, other])
        for t in range(NEED):
            stack[pl.ds(t * TILE + h * PART, PART)] = got[h][own_tab[0, t]]
    arrived(am.at[:, high], y_recv.at[2])
    arrived(ap.at[:, low], y_recv.at[3])
    arrived(ao.at[:, low], y_recv.at[4])
    arrived(ao.at[:, high], y_recv.at[5])

    square = jnp.zeros((8, LANES), jnp.float32)
    diagonal = lax.broadcasted_iota(jnp.int32, (rows, rows), 0) == lax.broadcasted_iota(jnp.int32, (rows, rows), 1)
    for dy, block in enumerate((a0, ap, ao, am)):
        ladder = jnp.dot(block[...], stack[...], preferred_element_type=jnp.float32)
        occ_rows = jnp.sum(jnp.where(diagonal, occs[dy], 0.0), axis=1, keepdims=True)
        update = ladder / (occ_rows - virs[y])
        square = square + jnp.sum((update * update).reshape(rows // 8, 8, LANES), axis=0)
        if dy == 0:
            cols[y] = update
        else:
            mine[dy] = update
            send(mine.at[dy], cols.at[y], u_send.at[dy], u_recv.at[y], at(0, dy, 0, 0))

    spot = z * 2 + c
    sum1[spot] = square
    partners = [(dz, dc) for dz in (4, 3, 5, 2, 6, 1, 7, 0) for dc in (1, 0) if (dz, dc) != (0, 0)]
    for i, (dz, dc) in enumerate(partners):
        send(sum1.at[spot], sum1.at[spot], s_send.at[i], s1_recv.at[spot], at(0, 0, dz, dc))
    for dz, dc in partners:
        other = lax.rem(z + dz, NZ) * 2 + lax.rem(c + dc, 2)
        arrived(sum1.at[other], s1_recv.at[other])
    spot = x * NY + y
    sum2[spot] = jnp.sum(sum1[...], axis=0)
    partners = [(dx, dy) for dx in (2, 1, 3, 0) for dy in (2, 1, 3, 0) if (dx, dy) != (0, 0)]
    for i, (dx, dy) in enumerate(partners):
        send(sum2.at[spot], sum2.at[spot], s_send.at[15 + i], s2_recv.at[spot], at(dx, dy, 0, 0))
    for dy in (1, 2, 3):
        other = lax.rem(y + dy, NY)
        arrived(cols.at[other], u_recv.at[other])
    for k in range(NY):
        out[:, k * LANES:(k + 1) * LANES] = cols[k]
    for dx, dy in partners:
        other = lax.rem(x + dx, NX) * NY + lax.rem(y + dy, NY)
        arrived(sum2.at[other], s2_recv.at[other])
    whole = jnp.sum(jnp.sum(sum2[...], axis=0), axis=(0, 1), keepdims=True)
    rms[...] = jnp.sqrt(whole / total_entries)
    for copy in started:
        copy.wait_send()


def per_device(amplitudes, integrals, task_owner, task_slot, occ_pair, vir_pair):
    rows, depth = amplitudes.shape
    columns = integrals.shape[1]
    bf16, f32, i32 = jnp.bfloat16, jnp.float32, jnp.int32
    dma = pltpu.SemaphoreType.DMA

    def body(*refs):
        kernel(rows, float(rows * OWNERS * NY * columns), *refs)

    anywhere, vmem = pl.BlockSpec(memory_space=pltpu.HBM), pl.BlockSpec(memory_space=pltpu.VMEM)
    update, rms = pl.pallas_call(
        body,
        out_shape=(
            jax.ShapeDtypeStruct((rows, columns), f32),
            jax.ShapeDtypeStruct((1, 1), f32),
        ),
        in_specs=[anywhere, anywhere, anywhere, anywhere, anywhere, anywhere],
        out_specs=(vmem, vmem),
        scratch_shapes=[
            *[pltpu.VMEM((1, OWNERS * NEED), i32)] * 2,
            *[pltpu.VMEM((OWNERS, NEED), i32)] * 2,
            pltpu.VMEM((OWNERS, LANES), i32),
            pltpu.VMEM((8, LANES), i32),
            pltpu.SMEM((OWNERS, LANES), i32),
            pltpu.SMEM((8, LANES), i32),
            *[pltpu.VMEM((CD_DEV, PART, LANES), bf16)] * 10,
            *[pltpu.VMEM((2 * OWNERS, PART, LANES), bf16)] * 2,
            pltpu.VMEM((PARTS, 5, 7, 2, PART, LANES), bf16),
            pltpu.VMEM((PARTS, 24, 2, PART, LANES), bf16),
            *[pltpu.VMEM((rows, depth), bf16)] * 4,
            pltpu.VMEM((depth, LANES), bf16),
            pltpu.VMEM((NY, rows, LANES), f32),
            pltpu.VMEM((NY, rows, LANES), f32),
            pltpu.VMEM((NY, 1, rows), f32),
            pltpu.VMEM((NY, 1, LANES), f32),
            *[pltpu.VMEM((16, 8, LANES), f32)] * 2,
            dma((9,)),
            dma((2, 2, PARTS)), dma((2, 2, PARTS)),
            dma((6,)), dma((6,)),
            dma((PARTS, 5, 7)), dma((PARTS, 24)), dma((PARTS, NZ, 8)),
            dma((NY,)), dma((NY,)),
            dma((NY,)), dma((NY,)),
            dma((30,)), dma((16,)), dma((16,)),
        ],
        compiler_params=pltpu.CompilerParams(
            collective_id=0, has_side_effects=True, vmem_limit_bytes=56 << 20
        ),
        cost_estimate=pl.CostEstimate(
            flops=2 * rows * depth * columns, bytes_accessed=8 << 20, transcendentals=0
        ),
        name="ladder",
    )(
        task_owner.T,
        task_slot.T,
        integrals.reshape(CD_DEV, TILE, columns),
        amplitudes,
        occ_pair.reshape(1, rows),
        vir_pair.reshape(NY, 1, LANES),
    )
    return update, rms[0, 0]


def solution(mesh):
    placed = (P(("own", "grp"), None), P("own", None), P(), P(), P(("own", "grp")), P())
    return jax.shard_map(
        per_device,
        mesh=mesh,
        in_specs=placed,
        out_specs=(P(("own", "grp"), None), P()),
        check_vma=False,
    )
```

```python
import jax
import jax.numpy as jnp
from jax import lax
from jax.experimental import pallas as pl
from jax.experimental.pallas import tpu as pltpu
from jax.sharding import PartitionSpec as P

MESH = pl.DeviceIdType.MESH
TILE = 128
SIZES = (64, 64)
PARTS = len(SIZES)
STARTS = tuple(sum(SIZES[:h]) for h in range(PARTS))
CD_DEV = 24
NEED = 44
OWNERS = 64
NX, NY, NZ = 4, 4, 8
LANES = 128
SHIFTS = (0, -1, 1, -2, 2)
LINE = ((0, 0), (0, 1), (1, 0), (3, 0), (1, 1), (3, 1), (2, 0), (2, 1))
OPPOSITE = (0, 1, 3, 2)
GROUPS = (LINE[1:4], LINE[4:])
GROUP_ENTRIES = (18, 24)
FROM_UP3, FROM_DOWN3, FROM_UP4, FROM_DOWN4, ALL_FAR = 80, 48, 64, 72, 48
ARRIVING = 5 * 14 + ALL_FAR
PASSED_ON = 42


def place_of(dx, dc):
    return LINE.index((dx % NX, dc)) * 2


def place_of_opposite(dx):
    return OPPOSITE.index(dx % NX) * 2


def fill_tables(own, x, z, c, owner_row, slot_row, owners, slots, table, takes):
    for reader in range(OWNERS):
        listed = slice(reader * NEED, (reader + 1) * NEED)
        owners[reader:reader + 1, :] = owner_row[0:1, listed]
        slots[reader:reader + 1, :] = slot_row[0:1, listed]
    lane = lax.broadcasted_iota(jnp.int32, (OWNERS, LANES), 1)
    filled = jnp.zeros((OWNERS, LANES), jnp.int32)
    for k, shift in enumerate(SHIFTS):
        source = x * 16 + lax.rem(z + shift + NZ, NZ) * 2 + c
        same = owners[...] == source
        first = jnp.min(jnp.where(same, slots[...], CD_DEV - 1), axis=1, keepdims=True)
        last = jnp.max(jnp.where(same, slots[...], 0), axis=1, keepdims=True)
        filled = jnp.where(lane == 2 * k, first, filled)
        filled = jnp.where(lane == 2 * k + 1, last, filled)
    table[...] = filled
    mine, wanted = owners[pl.ds(own, 1), :], slots[pl.ds(own, 1), :]
    square = (NEED, NEED)
    diagonal = lax.broadcasted_iota(jnp.int32, square, 0) == lax.broadcasted_iota(jnp.int32, square, 1)
    down_mine = jnp.sum(jnp.where(diagonal, mine, 0), axis=1, keepdims=True)
    down_wanted = jnp.sum(jnp.where(diagonal, wanted, 0), axis=1, keepdims=True)
    least = jnp.min(jnp.where(down_mine == mine, down_wanted, CD_DEV), axis=0, keepdims=True)
    second = (wanted > least).astype(jnp.int32)
    phase = (lax.shift_right_logical(mine, 1) - z + NZ) & 7
    dx = (lax.shift_right_logical(mine, 4) - x + NX) & 3
    dc = (mine + c) & 1
    near, far = jnp.zeros_like(mine), jnp.zeros_like(mine)
    for i, (step, core) in enumerate(LINE):
        near = jnp.where((dx == step) & (dc == core), 2 * i, near)
    for i, step in enumerate(OPPOSITE):
        far = jnp.where(dx == step, 2 * i, far)
    place = phase * 16 + jnp.where(phase == 4, far + 8 * dc, near) + second
    takes[...] = jnp.zeros(takes.shape, jnp.int32)
    takes[:, 0:NEED] = jnp.broadcast_to(place, (8, NEED))


def kernel(
    rows, total_entries, owner_list, slot_list, integ, amp, occ, vir, out, rms,
    owner_row, slot_row, owners, slots, table, takes, tab, own_tab, *refs,
):
    g0, gm1, gp1, gm2, gp2, got, sx, sd, up3, up4, down3, down4 = [refs[i * PARTS:(i + 1) * PARTS] for i in range(12)]
    (
        a0, am, ap, ao, stack, gaps, mine, cols, occs, virs, sum1, sum2, load_sem, quarter_sem,
        z_send, z_recv, y_send, y_recv, x_send, d_send, f_send, relay_recv, got_recv,
        occ_sem, u_sem, s_send, s_recv,
    ) = refs[12 * PARTS:]
    own, y = lax.axis_index("own"), lax.axis_index("grp")
    x, z, c = lax.div(own, 16), lax.rem(lax.div(own, 2), 8), lax.rem(own, 2)
    half = amp.shape[1] // 2

    def at(dx=0, dy=0, dz=0, dc=0):
        nx, nz = lax.rem(x + dx + NX, NX), lax.rem(z + dz + NZ, NZ)
        return (nx * 16 + nz * 2 + lax.rem(c + dc, 2), lax.rem(y + dy + NY, NY))

    def send(src, dst, send_sem, recv_sem, device):
        copy = pltpu.make_async_remote_copy(
            src_ref=src, dst_ref=dst, send_sem=send_sem, recv_sem=recv_sem,
            device_id=device, device_id_type=MESH,
        )
        copy.start()
        return copy

    def whole(ref, sem):
        return pltpu.make_async_remote_copy(
            src_ref=ref, dst_ref=ref, send_sem=sem, recv_sem=sem,
            device_id=at(0, 0, 1, 0), device_id_type=MESH,
        )

    def arrived(ref, sem):
        whole(ref, sem).wait_recv()

    def left_here(ref, sem):
        whole(ref, sem).wait_send()

    barrier = pltpu.get_barrier_semaphore()
    targets = [(0, 0, 1, 0), (0, 0, -1, 0)] + [(dx, 0, 0, dc) for dx, dc in LINE[1:]] + [(0, dy, 0, 0) for dy in (1, 2, 3)]
    for dx, dy, dz, dc in targets:
        pl.semaphore_signal(barrier, inc=1, device_id=at(-dx, -dy, -dz, dc), device_id_type=MESH)

    loads = [
        pltpu.make_async_copy(
            integ.at[:, pl.ds(STARTS[h], SIZES[h]), pl.ds(pl.multiple_of(y * LANES, LANES), LANES)],
            g0[h], quarter_sem.at[h])
        for h in range(PARTS)
    ]
    loads.append(pltpu.make_async_copy(amp, a0, load_sem.at[0]))
    loads.append(pltpu.make_async_copy(occ, occs.at[0], load_sem.at[1]))
    loads.append(pltpu.make_async_copy(vir, virs, load_sem.at[2]))
    loads.append(pltpu.make_async_copy(owner_list, owner_row, load_sem.at[3]))
    loads.append(pltpu.make_async_copy(slot_list, slot_row, load_sem.at[4]))
    for copy in loads:
        copy.start()
    loads[0].wait()
    pl.semaphore_wait(barrier, len(targets))

    right, left = at(0, 0, 1, 0), at(0, 0, -1, 0)
    low, high = pl.ds(0, half), pl.ds(half, half)
    up, down = at(0, 1, 0, 0), at(0, -1, 0, 0)

    def pick(block, k, r, reader):
        return block[tab[reader, 2 * k + r]]

    def across(k, h, block):
        first = SHIFTS[k] % NZ * 16
        for i, (dx, dc) in enumerate(LINE[1:]):
            device = at(dx, 0, 0, dc)
            for r in range(2):
                sx[h][k, i, r] = pick(block, k, r, device[0])
            place = pl.ds(first + place_of(-dx, dc), 2)
            send(sx[h].at[k, i], got[h].at[place], x_send.at[h], got_recv.at[h], device)
        for r in range(2):
            got[h][first + r] = pick(block, k, r, own)

    def relay(k, h, block, slot, dz, dx, dc, meet, place, target):
        reader = at(dx, 0, dz, dc)[0]
        for r in range(2):
            sd[h][slot, r] = pick(block, k, r, reader)
        if (dx, dc) == (0, 0):
            send(sd[h].at[slot], got[h].at[pl.ds(target, 2)], d_send.at[h], got_recv.at[h], at(0, 0, dz, 0))
        else:
            group = 0 if (dx, dc) in GROUPS[0] else 1
            send(sd[h].at[slot], meet.at[pl.ds(place, 2)], d_send.at[h], relay_recv.at[h, group], at(dx, 0, 0, dc))

    def far(h):
        for i, (dx, dc) in enumerate(LINE):
            place, place4 = place_of(-dx, dc), place_of_opposite(-dx)
            if dc == 0:
                relay(3, h, gm2[h], 16 + dx, 2, dx, 0, up4[h], place4, FROM_UP4)
            else:
                relay(4, h, gp2[h], 20 + dx, -2, dx, 1, down4[h], place4, FROM_DOWN4)
            relay(3, h, gm2[h], i, 1, dx, dc, up3[h], place, FROM_UP3)
            relay(4, h, gp2[h], 8 + i, -1, dx, dc, down3[h], place, FROM_DOWN3)

    def onward(h, group):
        arrived(got[h].at[pl.ds(0, GROUP_ENTRIES[group])], relay_recv.at[h, group])
        lines = ((2, 6), (8, 8))[group]
        straight, crossed = ((2, 4), (6, 2))[group], ((0, 2), (2, 6))[group]
        for block, (first, count), target, device in (
            (up4[h], straight, FROM_UP4, at(0, 0, 2, 0)),
            (down4[h], crossed, FROM_DOWN4, at(0, 0, -2, 0)),
            (up3[h], lines, FROM_UP3, right),
            (down3[h], lines, FROM_DOWN3, left),
        ):
            send(block.at[pl.ds(first, count)], got[h].at[pl.ds(target + first, count)], f_send.at[h], got_recv.at[h], device)

    def first_hop(h):
        return (
            send(g0[h], gm1[h], z_send.at[0, 0, h], z_recv.at[0, 0, h], right),
            send(g0[h], gp1[h], z_send.at[1, 0, h], z_recv.at[1, 0, h], left),
        )

    def second_hop(h):
        arrived(gm1[h], z_recv.at[0, 0, h])
        onto = send(gm1[h], gm2[h], z_send.at[0, 1, h], z_recv.at[0, 1, h], right)
        arrived(gp1[h], z_recv.at[1, 0, h])
        return onto, send(gp1[h], gp2[h], z_send.at[1, 1, h], z_recv.at[1, 1, h], left)

    def come(h):
        arrived(gm2[h], z_recv.at[0, 1, h])
        arrived(gp2[h], z_recv.at[1, 1, h])

    def across_two(h):
        across(3, h, gm2[h])
        across(4, h, gp2[h])

    waiting = []
    first = first_hop(0)
    first_rows = (
        send(amp.at[:, low], am.at[:, low], y_send.at[0], y_recv.at[0], up),
        send(amp.at[:, high], ap.at[:, high], y_send.at[1], y_recv.at[1], down),
    )
    for copy in loads[1:]:
        copy.wait()
    for dy in (1, 2, 3):
        send(occs.at[0], occs.at[NY - dy], occ_sem.at[0], occ_sem.at[1], at(0, dy, 0, 0))
    fill_tables(own, x, z, c, owner_row, slot_row, owners, slots, table, takes)
    to_scalar = (pltpu.make_async_copy(table, tab, load_sem.at[5]), pltpu.make_async_copy(takes, own_tab, load_sem.at[6]))
    for copy in to_scalar:
        copy.start()
    for copy in to_scalar:
        copy.wait()
    across(0, 0, g0[0])
    for h in range(1, PARTS):
        for copy in first:
            copy.wait_send()
        first = first_hop(h)
        across(0, h, g0[h])
        waiting += second_hop(h - 1)
        across(1, h - 1, gm1[h - 1])
        across(2, h - 1, gp1[h - 1])
    waiting += first
    for copy in first_rows:
        copy.wait_send()
    waiting.append(send(a0.at[:, high], am.at[:, high], y_send.at[2], y_recv.at[2], up))
    waiting.append(send(a0.at[:, low], ap.at[:, low], y_send.at[3], y_recv.at[3], down))
    waiting += second_hop(PARTS - 1)
    arrived(am.at[:, low], y_recv.at[0])
    waiting.append(send(am.at[:, low], ao.at[:, low], y_send.at[4], y_recv.at[4], up))
    arrived(ap.at[:, high], y_recv.at[1])
    waiting.append(send(ap.at[:, high], ao.at[:, high], y_send.at[5], y_recv.at[5], down))
    across(1, PARTS - 1, gm1[PARTS - 1])
    across(2, PARTS - 1, gp1[PARTS - 1])
    come(0)
    far(0)
    for h in range(1, PARTS):
        onward(h - 1, 0)
        come(h)
        far(h)
        onward(h - 1, 1)
        across_two(h - 1)
    onward(PARTS - 1, 0)
    across_two(PARTS - 1)
    onward(PARTS - 1, 1)

    arrived(occs.at[pl.ds(0, 3)], occ_sem.at[1])
    diagonal = lax.broadcasted_iota(jnp.int32, (rows, rows), 0) == lax.broadcasted_iota(jnp.int32, (rows, rows), 1)
    for dy in range(NY):
        occ_rows = jnp.sum(jnp.where(diagonal, occs[dy], 0.0), axis=1, keepdims=True)
        gaps[dy] = occ_rows - virs[y]
    for h in range(PARTS):
        arrived(got[h].at[pl.ds(0, ARRIVING)], got_recv.at[h])
        for t in range(NEED):
            stack[pl.ds(t * TILE + STARTS[h], SIZES[h])] = got[h][own_tab[0, t]]
    arrived(am.at[:, high], y_recv.at[2])
    arrived(ap.at[:, low], y_recv.at[3])
    arrived(ao.at[:, low], y_recv.at[4])
    arrived(ao.at[:, high], y_recv.at[5])

    square = jnp.zeros((8, LANES), jnp.float32)
    for dy, block in enumerate((a0, ap, ao, am)):
        ladder = jnp.dot(block[...], stack[...], preferred_element_type=jnp.float32)
        update = ladder / gaps[dy]
        square = square + jnp.sum((update * update).reshape(rows // 8, 8, LANES), axis=0)
        if dy == 0:
            cols[y] = update
        else:
            mine[dy] = update

    spot = z * 2 + c
    sum1[spot] = square
    for dz in (4, 3, 5, 2, 6, 1, 7, 0):
        for dc in (1, 0):
            if (dz, dc) != (0, 0):
                send(sum1.at[spot], sum1.at[spot], s_send.at[0], s_recv.at[0], at(0, 0, dz, dc))
    for dy in (1, 2, 3):
        send(mine.at[dy], cols.at[y], u_sem.at[0], u_sem.at[1], at(0, dy, 0, 0))
    for copy in waiting:
        copy.wait_send()
    left_here(occs.at[pl.ds(0, 3)], occ_sem.at[0])
    for h in range(PARTS):
        left_here(sx[h], x_send.at[h])
        left_here(sd[h], d_send.at[h])
        left_here(got[h].at[pl.ds(0, PASSED_ON)], f_send.at[h])
    arrived(sum1.at[pl.ds(0, 15)], s_recv.at[0])
    spot = x * NY + y
    sum2[spot] = jnp.sum(sum1[...], axis=0)
    for dx in (2, 1, 3, 0):
        for dy in (2, 1, 3, 0):
            if (dx, dy) != (0, 0):
                send(sum2.at[spot], sum2.at[spot], s_send.at[1], s_recv.at[1], at(dx, dy, 0, 0))
    left_here(sum1.at[pl.ds(0, 15)], s_send.at[0])
    arrived(cols.at[pl.ds(0, 3)], u_sem.at[1])
    stores = []
    for k in range(NY):
        stores.append(pltpu.make_async_copy(cols.at[k], out.at[:, pl.ds(k * LANES, LANES)], load_sem.at[k]))
        stores[k].start()
    left_here(cols.at[pl.ds(0, 3)], u_sem.at[0])
    arrived(sum2.at[pl.ds(0, 15)], s_recv.at[1])
    everything = jnp.sum(jnp.sum(sum2[...], axis=0), axis=(0, 1), keepdims=True)
    rms[...] = jnp.sqrt(everything / total_entries)
    for copy in stores:
        copy.wait()
    left_here(sum2.at[pl.ds(0, 15)], s_send.at[1])


def per_device(amplitudes, integrals, task_owner, task_slot, occ_pair, vir_pair):
    rows, depth = amplitudes.shape
    columns = integrals.shape[1]
    bf16, f32, i32 = jnp.bfloat16, jnp.float32, jnp.int32
    dma = pltpu.SemaphoreType.DMA

    def body(*refs):
        kernel(rows, float(rows * OWNERS * NY * columns), *refs)

    def parts(*lead):
        return [pltpu.VMEM((*lead, size, LANES), bf16) for size in SIZES]

    anywhere, vmem = pl.BlockSpec(memory_space=pltpu.HBM), pl.BlockSpec(memory_space=pltpu.VMEM)
    update, rms = pl.pallas_call(
        body,
        out_shape=(
            jax.ShapeDtypeStruct((rows, columns), f32),
            jax.ShapeDtypeStruct((1, 1), f32),
        ),
        in_specs=[anywhere] * 6,
        out_specs=(anywhere, vmem),
        scratch_shapes=[
            *[pltpu.VMEM((1, OWNERS * NEED), i32)] * 2,
            *[pltpu.VMEM((OWNERS, NEED), i32)] * 2,
            pltpu.VMEM((OWNERS, LANES), i32),
            pltpu.VMEM((8, LANES), i32),
            pltpu.SMEM((OWNERS, LANES), i32),
            pltpu.SMEM((8, LANES), i32),
            *parts(CD_DEV), *parts(CD_DEV), *parts(CD_DEV), *parts(CD_DEV), *parts(CD_DEV),
            *parts(2 * OWNERS), *parts(5, 7, 2), *parts(24, 2),
            *parts(16), *parts(8), *parts(16), *parts(8),
            *[pltpu.VMEM((rows, depth), bf16)] * 4,
            pltpu.VMEM((depth, LANES), bf16),
            *[pltpu.VMEM((NY, rows, LANES), f32)] * 3,
            pltpu.VMEM((NY, 1, rows), f32),
            pltpu.VMEM((NY, 1, LANES), f32),
            *[pltpu.VMEM((16, 8, LANES), f32)] * 2,
            dma((7,)), dma((PARTS,)),
            dma((2, 2, PARTS)), dma((2, 2, PARTS)),
            dma((6,)), dma((6,)),
            dma((PARTS,)), dma((PARTS,)), dma((PARTS,)), dma((PARTS, 2)), dma((PARTS,)),
            dma((2,)), dma((2,)), dma((2,)), dma((2,)),
        ],
        compiler_params=pltpu.CompilerParams(
            collective_id=0, has_side_effects=True, vmem_limit_bytes=56 << 20
        ),
        cost_estimate=pl.CostEstimate(
            flops=2 * rows * depth * columns, bytes_accessed=8 << 20, transcendentals=0
        ),
        name="ladder",
    )(
        task_owner.T,
        task_slot.T,
        integrals.reshape(CD_DEV, TILE, columns),
        amplitudes,
        occ_pair.reshape(1, rows),
        vir_pair.reshape(NY, 1, LANES),
    )
    return update, rms[0, 0]


def solution(mesh):
    placed = (P(("own", "grp"), None), P("own", None), P(), P(), P(("own", "grp")), P())
    return jax.shard_map(
        per_device,
        mesh=mesh,
        in_specs=placed,
        out_specs=(P(("own", "grp"), None), P()),
        check_vma=False,
    )
```

```python
import jax
import jax.numpy as jnp
from jax import lax
from jax.experimental import pallas as pl
from jax.experimental.pallas import tpu as pltpu
from jax.sharding import PartitionSpec as P

MESH = pl.DeviceIdType.MESH
TILE = 128
SIZES = (64, 64)
PARTS = len(SIZES)
STARTS = tuple(sum(SIZES[:h]) for h in range(PARTS))
CD_DEV = 24
NEED = 44
OWNERS = 64
NX, NY, NZ = 4, 4, 8
LANES = 128
SHIFTS = (0, -1, 1, -2, 2)
LINE = ((0, 0), (0, 1), (1, 0), (3, 0), (1, 1), (3, 1), (2, 0), (2, 1))
OPPOSITE = (0, 1, 3, 2)
GROUPS = (LINE[1:4], LINE[4:])
GROUP_ENTRIES = (18, 24)
FROM_UP3, FROM_DOWN3, FROM_UP4, FROM_DOWN4, ALL_FAR = 80, 48, 64, 72, 48
ARRIVING = 5 * 14 + ALL_FAR
PASSED_ON = 42


def place_of(dx, dc):
    return LINE.index((dx % NX, dc)) * 2


def place_of_opposite(dx):
    return OPPOSITE.index(dx % NX) * 2


def fill_tables(own, x, z, c, owner_row, slot_row, owners, slots, table, takes):
    for reader in range(OWNERS):
        listed = slice(reader * NEED, (reader + 1) * NEED)
        owners[reader:reader + 1, :] = owner_row[0:1, listed]
        slots[reader:reader + 1, :] = slot_row[0:1, listed]
    lane = lax.broadcasted_iota(jnp.int32, (OWNERS, LANES), 1)
    filled = jnp.zeros((OWNERS, LANES), jnp.int32)
    for k, shift in enumerate(SHIFTS):
        source = x * 16 + lax.rem(z + shift + NZ, NZ) * 2 + c
        same = owners[...] == source
        first = jnp.min(jnp.where(same, slots[...], CD_DEV - 1), axis=1, keepdims=True)
        last = jnp.max(jnp.where(same, slots[...], 0), axis=1, keepdims=True)
        filled = jnp.where(lane == 2 * k, first, filled)
        filled = jnp.where(lane == 2 * k + 1, last, filled)
    table[...] = filled
    mine, wanted = owners[pl.ds(own, 1), :], slots[pl.ds(own, 1), :]
    square = (NEED, NEED)
    diagonal = lax.broadcasted_iota(jnp.int32, square, 0) == lax.broadcasted_iota(jnp.int32, square, 1)
    down_mine = jnp.sum(jnp.where(diagonal, mine, 0), axis=1, keepdims=True)
    down_wanted = jnp.sum(jnp.where(diagonal, wanted, 0), axis=1, keepdims=True)
    least = jnp.min(jnp.where(down_mine == mine, down_wanted, CD_DEV), axis=0, keepdims=True)
    second = (wanted > least).astype(jnp.int32)
    phase = (lax.shift_right_logical(mine, 1) - z + NZ) & 7
    dx = (lax.shift_right_logical(mine, 4) - x + NX) & 3
    dc = (mine + c) & 1
    near, far = jnp.zeros_like(mine), jnp.zeros_like(mine)
    for i, (step, core) in enumerate(LINE):
        near = jnp.where((dx == step) & (dc == core), 2 * i, near)
    for i, step in enumerate(OPPOSITE):
        far = jnp.where(dx == step, 2 * i, far)
    place = phase * 16 + jnp.where(phase == 4, far + 8 * dc, near) + second
    takes[...] = jnp.zeros(takes.shape, jnp.int32)
    takes[:, 0:NEED] = jnp.broadcast_to(place, (8, NEED))


def kernel(
    rows, total_entries, owner_list, slot_list, integ, amp, occ, vir, out, rms,
    owner_row, slot_row, owners, slots, table, takes, tab, own_tab, *refs,
):
    g0, gm1, gp1, gm2, gp2, got, sx, sd, up3, up4, down3, down4 = [refs[i * PARTS:(i + 1) * PARTS] for i in range(12)]
    (
        a0, am, ap, ao, stack, gaps, mine, cols, occs, virs, sum1, sum2, load_sem, quarter_sem,
        z_send, z_recv, y_send, y_recv, x_send, d_send, f_send, relay_recv, got_recv,
        occ_sem, u_sem, s_send, s_recv,
    ) = refs[12 * PARTS:]
    own, y = lax.axis_index("own"), lax.axis_index("grp")
    x, z, c = lax.div(own, 16), lax.rem(lax.div(own, 2), 8), lax.rem(own, 2)
    half = amp.shape[1] // 2

    def at(dx=0, dy=0, dz=0, dc=0):
        nx, nz = lax.rem(x + dx + NX, NX), lax.rem(z + dz + NZ, NZ)
        return (nx * 16 + nz * 2 + lax.rem(c + dc, 2), lax.rem(y + dy + NY, NY))

    def send(src, dst, send_sem, recv_sem, device):
        copy = pltpu.make_async_remote_copy(
            src_ref=src, dst_ref=dst, send_sem=send_sem, recv_sem=recv_sem,
            device_id=device, device_id_type=MESH,
        )
        copy.start()
        return copy

    def whole(ref, sem):
        return pltpu.make_async_remote_copy(
            src_ref=ref, dst_ref=ref, send_sem=sem, recv_sem=sem,
            device_id=at(0, 0, 1, 0), device_id_type=MESH,
        )

    def arrived(ref, sem):
        whole(ref, sem).wait_recv()

    def left_here(ref, sem):
        whole(ref, sem).wait_send()

    loads = [
        pltpu.make_async_copy(
            integ.at[:, pl.ds(STARTS[h], SIZES[h]), pl.ds(pl.multiple_of(y * LANES, LANES), LANES)],
            g0[h], quarter_sem.at[h])
        for h in range(PARTS)
    ]
    loads.append(pltpu.make_async_copy(amp, a0, load_sem.at[0]))
    loads.append(pltpu.make_async_copy(occ, occs.at[0], load_sem.at[1]))
    loads.append(pltpu.make_async_copy(vir, virs, load_sem.at[2]))
    loads.append(pltpu.make_async_copy(owner_list, owner_row, load_sem.at[3]))
    loads.append(pltpu.make_async_copy(slot_list, slot_row, load_sem.at[4]))
    for copy in loads:
        copy.start()
    barrier = pltpu.get_barrier_semaphore()
    targets = [(0, 0, 1, 0), (0, 0, -1, 0)] + [(dx, 0, 0, dc) for dx, dc in LINE[1:]] + [(0, dy, 0, 0) for dy in (1, 2, 3)]
    for dx, dy, dz, dc in targets:
        pl.semaphore_signal(barrier, inc=1, device_id=at(-dx, -dy, -dz, dc), device_id_type=MESH)
    loads[0].wait()
    pl.semaphore_wait(barrier, len(targets))

    right, left = at(0, 0, 1, 0), at(0, 0, -1, 0)
    low, high = pl.ds(0, half), pl.ds(half, half)
    up, down = at(0, 1, 0, 0), at(0, -1, 0, 0)

    def pick(block, k, r, reader):
        return block[tab[reader, 2 * k + r]]

    def across(k, h, block):
        first = SHIFTS[k] % NZ * 16
        for i, (dx, dc) in enumerate(LINE[1:]):
            device = at(dx, 0, 0, dc)
            for r in range(2):
                sx[h][k, i, r] = pick(block, k, r, device[0])
            place = pl.ds(first + place_of(-dx, dc), 2)
            send(sx[h].at[k, i], got[h].at[place], x_send.at[h], got_recv.at[h], device)
        for r in range(2):
            got[h][first + r] = pick(block, k, r, own)

    def relay(k, h, block, slot, dz, dx, dc, meet, place, target):
        reader = at(dx, 0, dz, dc)[0]
        for r in range(2):
            sd[h][slot, r] = pick(block, k, r, reader)
        if (dx, dc) == (0, 0):
            send(sd[h].at[slot], got[h].at[pl.ds(target, 2)], d_send.at[h], got_recv.at[h], at(0, 0, dz, 0))
        else:
            group = 0 if (dx, dc) in GROUPS[0] else 1
            send(sd[h].at[slot], meet.at[pl.ds(place, 2)], d_send.at[h], relay_recv.at[h, group], at(dx, 0, 0, dc))

    def far(h):
        for i, (dx, dc) in enumerate(LINE):
            place, place4 = place_of(-dx, dc), place_of_opposite(-dx)
            if dc == 0:
                relay(3, h, gm2[h], 16 + dx, 2, dx, 0, up4[h], place4, FROM_UP4)
            else:
                relay(4, h, gp2[h], 20 + dx, -2, dx, 1, down4[h], place4, FROM_DOWN4)
            relay(3, h, gm2[h], i, 1, dx, dc, up3[h], place, FROM_UP3)
            relay(4, h, gp2[h], 8 + i, -1, dx, dc, down3[h], place, FROM_DOWN3)

    def onward(h, group):
        arrived(got[h].at[pl.ds(0, GROUP_ENTRIES[group])], relay_recv.at[h, group])
        lines = ((2, 6), (8, 8))[group]
        straight, crossed = ((2, 4), (6, 2))[group], ((0, 2), (2, 6))[group]
        for block, (first, count), target, device in (
            (up4[h], straight, FROM_UP4, at(0, 0, 2, 0)),
            (down4[h], crossed, FROM_DOWN4, at(0, 0, -2, 0)),
            (up3[h], lines, FROM_UP3, right),
            (down3[h], lines, FROM_DOWN3, left),
        ):
            send(block.at[pl.ds(first, count)], got[h].at[pl.ds(target + first, count)], f_send.at[h], got_recv.at[h], device)

    def first_hop(h):
        return (
            send(g0[h], gm1[h], z_send.at[0, 0, h], z_recv.at[0, 0, h], right),
            send(g0[h], gp1[h], z_send.at[1, 0, h], z_recv.at[1, 0, h], left),
        )

    def second_hop(h):
        arrived(gm1[h], z_recv.at[0, 0, h])
        onto = send(gm1[h], gm2[h], z_send.at[0, 1, h], z_recv.at[0, 1, h], right)
        arrived(gp1[h], z_recv.at[1, 0, h])
        return onto, send(gp1[h], gp2[h], z_send.at[1, 1, h], z_recv.at[1, 1, h], left)

    def come(h):
        arrived(gm2[h], z_recv.at[0, 1, h])
        arrived(gp2[h], z_recv.at[1, 1, h])

    def across_two(h):
        across(3, h, gm2[h])
        across(4, h, gp2[h])

    waiting = [*first_hop(0)]
    for h in range(1, PARTS):
        loads[h].wait()
        waiting += first_hop(h)
    first_rows = (
        send(amp.at[:, low], am.at[:, low], y_send.at[0], y_recv.at[0], up),
        send(amp.at[:, high], ap.at[:, high], y_send.at[1], y_recv.at[1], down),
    )
    for copy in loads[PARTS:]:
        copy.wait()
    for dy in (1, 2, 3):
        send(occs.at[0], occs.at[NY - dy], occ_sem.at[0], occ_sem.at[1], at(0, dy, 0, 0))
    fill_tables(own, x, z, c, owner_row, slot_row, owners, slots, table, takes)
    to_scalar = (pltpu.make_async_copy(table, tab, load_sem.at[5]), pltpu.make_async_copy(takes, own_tab, load_sem.at[6]))
    for copy in to_scalar:
        copy.start()
    for copy in to_scalar:
        copy.wait()
    across(0, 0, g0[0])
    for h in range(1, PARTS):
        across(0, h, g0[h])
        waiting += second_hop(h - 1)
        across(1, h - 1, gm1[h - 1])
        across(2, h - 1, gp1[h - 1])
    for copy in first_rows:
        copy.wait_send()
    waiting.append(send(a0.at[:, high], am.at[:, high], y_send.at[2], y_recv.at[2], up))
    waiting.append(send(a0.at[:, low], ap.at[:, low], y_send.at[3], y_recv.at[3], down))
    waiting += second_hop(PARTS - 1)
    arrived(am.at[:, low], y_recv.at[0])
    waiting.append(send(am.at[:, low], ao.at[:, low], y_send.at[4], y_recv.at[4], up))
    arrived(ap.at[:, high], y_recv.at[1])
    waiting.append(send(ap.at[:, high], ao.at[:, high], y_send.at[5], y_recv.at[5], down))
    across(1, PARTS - 1, gm1[PARTS - 1])
    across(2, PARTS - 1, gp1[PARTS - 1])
    come(0)
    far(0)
    for h in range(1, PARTS):
        onward(h - 1, 0)
        come(h)
        far(h)
        onward(h - 1, 1)
        across_two(h - 1)
    onward(PARTS - 1, 0)
    across_two(PARTS - 1)
    onward(PARTS - 1, 1)

    arrived(occs.at[pl.ds(0, 3)], occ_sem.at[1])
    diagonal = lax.broadcasted_iota(jnp.int32, (rows, rows), 0) == lax.broadcasted_iota(jnp.int32, (rows, rows), 1)
    for dy in range(NY):
        occ_rows = jnp.sum(jnp.where(diagonal, occs[dy], 0.0), axis=1, keepdims=True)
        gaps[dy] = occ_rows - virs[y]
    for h in range(PARTS):
        arrived(got[h].at[pl.ds(0, ARRIVING)], got_recv.at[h])
        for t in range(NEED):
            stack[pl.ds(t * TILE + STARTS[h], SIZES[h])] = got[h][own_tab[0, t]]
    arrived(am.at[:, high], y_recv.at[2])
    arrived(ap.at[:, low], y_recv.at[3])
    arrived(ao.at[:, low], y_recv.at[4])
    arrived(ao.at[:, high], y_recv.at[5])

    square = jnp.zeros((8, LANES), jnp.float32)
    for dy, block in enumerate((a0, ap, ao, am)):
        ladder = jnp.dot(block[...], stack[...], preferred_element_type=jnp.float32)
        update = ladder / gaps[dy]
        square = square + jnp.sum((update * update).reshape(rows // 8, 8, LANES), axis=0)
        if dy == 0:
            cols[y] = update
        else:
            mine[dy] = update

    spot = z * 2 + c
    sum1[spot] = jnp.sum(square, axis=0, keepdims=True)
    for dz in (4, 3, 5, 2, 6, 1, 7, 0):
        for dc in (1, 0):
            if (dz, dc) != (0, 0):
                send(sum1.at[spot], sum1.at[spot], s_send.at[0], s_recv.at[0], at(0, 0, dz, dc))
    for dy in (1, 2, 3):
        send(mine.at[dy], cols.at[y], u_sem.at[0], u_sem.at[1], at(0, dy, 0, 0))
    for copy in waiting:
        copy.wait_send()
    left_here(occs.at[pl.ds(0, 3)], occ_sem.at[0])
    for h in range(PARTS):
        left_here(sx[h], x_send.at[h])
        left_here(sd[h], d_send.at[h])
        left_here(got[h].at[pl.ds(0, PASSED_ON)], f_send.at[h])
    arrived(sum1.at[pl.ds(0, 15)], s_recv.at[0])
    spot = x * NY + y
    sum2[spot] = jnp.sum(sum1[...], axis=0)
    for dx in (2, 1, 3, 0):
        for dy in (2, 1, 3, 0):
            if (dx, dy) != (0, 0):
                send(sum2.at[spot], sum2.at[spot], s_send.at[1], s_recv.at[1], at(dx, dy, 0, 0))
    left_here(sum1.at[pl.ds(0, 15)], s_send.at[0])
    arrived(cols.at[pl.ds(0, 3)], u_sem.at[1])
    stores = []
    for k in range(NY):
        stores.append(pltpu.make_async_copy(cols.at[k], out.at[:, pl.ds(k * LANES, LANES)], load_sem.at[k]))
        stores[k].start()
    left_here(cols.at[pl.ds(0, 3)], u_sem.at[0])
    arrived(sum2.at[pl.ds(0, 15)], s_recv.at[1])
    everything = jnp.sum(jnp.sum(sum2[...], axis=0), axis=1, keepdims=True)
    rms[...] = jnp.sqrt(everything / total_entries)
    for copy in stores:
        copy.wait()
    left_here(sum2.at[pl.ds(0, 15)], s_send.at[1])


def per_device(amplitudes, integrals, task_owner, task_slot, occ_pair, vir_pair):
    rows, depth = amplitudes.shape
    columns = integrals.shape[1]
    bf16, f32, i32 = jnp.bfloat16, jnp.float32, jnp.int32
    dma = pltpu.SemaphoreType.DMA

    def body(*refs):
        kernel(rows, float(rows * OWNERS * NY * columns), *refs)

    def parts(*lead):
        return [pltpu.VMEM((*lead, size, LANES), bf16) for size in SIZES]

    anywhere, vmem = pl.BlockSpec(memory_space=pltpu.HBM), pl.BlockSpec(memory_space=pltpu.VMEM)
    update, rms = pl.pallas_call(
        body,
        out_shape=(
            jax.ShapeDtypeStruct((rows, columns), f32),
            jax.ShapeDtypeStruct((1, 1), f32),
        ),
        in_specs=[anywhere] * 6,
        out_specs=(anywhere, vmem),
        scratch_shapes=[
            *[pltpu.VMEM((1, OWNERS * NEED), i32)] * 2,
            *[pltpu.VMEM((OWNERS, NEED), i32)] * 2,
            pltpu.VMEM((OWNERS, LANES), i32),
            pltpu.VMEM((8, LANES), i32),
            pltpu.SMEM((OWNERS, LANES), i32),
            pltpu.SMEM((8, LANES), i32),
            *parts(CD_DEV), *parts(CD_DEV), *parts(CD_DEV), *parts(CD_DEV), *parts(CD_DEV),
            *parts(2 * OWNERS), *parts(5, 7, 2), *parts(24, 2),
            *parts(16), *parts(8), *parts(16), *parts(8),
            *[pltpu.VMEM((rows, depth), bf16)] * 4,
            pltpu.VMEM((depth, LANES), bf16),
            *[pltpu.VMEM((NY, rows, LANES), f32)] * 3,
            pltpu.VMEM((NY, 1, rows), f32),
            pltpu.VMEM((NY, 1, LANES), f32),
            *[pltpu.VMEM((16, 1, LANES), f32)] * 2,
            dma((7,)), dma((PARTS,)),
            dma((2, 2, PARTS)), dma((2, 2, PARTS)),
            dma((6,)), dma((6,)),
            dma((PARTS,)), dma((PARTS,)), dma((PARTS,)), dma((PARTS, 2)), dma((PARTS,)),
            dma((2,)), dma((2,)), dma((2,)), dma((2,)),
        ],
        compiler_params=pltpu.CompilerParams(
            collective_id=0, has_side_effects=True, vmem_limit_bytes=56 << 20
        ),
        cost_estimate=pl.CostEstimate(
            flops=2 * rows * depth * columns, bytes_accessed=8 << 20, transcendentals=0
        ),
        name="ladder",
    )(
        task_owner.T,
        task_slot.T,
        integrals.reshape(CD_DEV, TILE, columns),
        amplitudes,
        occ_pair.reshape(1, rows),
        vir_pair.reshape(NY, 1, LANES),
    )
    return update, rms[0, 0]


def solution(mesh):
    placed = (P(("own", "grp"), None), P("own", None), P(), P(), P(("own", "grp")), P())
    return jax.shard_map(
        per_device,
        mesh=mesh,
        in_specs=placed,
        out_specs=(P(("own", "grp"), None), P()),
        check_vma=False,
    )
```

```python
import jax
import jax.numpy as jnp
from jax import lax
from jax.experimental import pallas as pl
from jax.experimental.pallas import tpu as pltpu
from jax.sharding import PartitionSpec as P

MESH = pl.DeviceIdType.MESH
TILE = 128
PART = 64
SIZES = (PART, PART)
PARTS = len(SIZES)
STARTS = tuple(sum(SIZES[:h]) for h in range(PARTS))
CD_DEV = 24
NEED = 44
OWNERS = 64
NX, NY, NZ = 4, 4, 8
LANES = 128
SHIFTS = (0, -1, 1, -2, 2)
LINE = ((0, 0), (0, 1), (1, 0), (3, 0), (1, 1), (3, 1), (2, 0), (2, 1))
OPPOSITE = (0, 1, 3, 2)
GROUPS = (LINE[1:4], LINE[4:])
GROUP_ENTRIES = (18, 24)
FROM_UP3, FROM_DOWN3, FROM_UP4, FROM_DOWN4, ALL_FAR = 80, 48, 64, 72, 48
ARRIVING = 5 * 14 + ALL_FAR
PASSED_ON = 42


def place_of(dx, dc):
    return LINE.index((dx % NX, dc)) * 2


def place_of_opposite(dx):
    return OPPOSITE.index(dx % NX) * 2


def fill_tables(own, x, z, c, owner_row, slot_row, owners, slots, table, takes):
    for reader in range(OWNERS):
        listed = slice(reader * NEED, (reader + 1) * NEED)
        owners[reader:reader + 1, :] = owner_row[0:1, listed]
        slots[reader:reader + 1, :] = slot_row[0:1, listed]
    lane = lax.broadcasted_iota(jnp.int32, (OWNERS, LANES), 1)
    filled = jnp.zeros((OWNERS, LANES), jnp.int32)
    for k, shift in enumerate(SHIFTS):
        source = x * 16 + lax.rem(z + shift + NZ, NZ) * 2 + c
        same = owners[...] == source
        first = jnp.min(jnp.where(same, slots[...], CD_DEV - 1), axis=1, keepdims=True)
        last = jnp.max(jnp.where(same, slots[...], 0), axis=1, keepdims=True)
        filled = jnp.where(lane == 2 * k, first, filled)
        filled = jnp.where(lane == 2 * k + 1, last, filled)
    table[...] = filled
    mine, wanted = owners[pl.ds(own, 1), :], slots[pl.ds(own, 1), :]
    square = (NEED, NEED)
    diagonal = lax.broadcasted_iota(jnp.int32, square, 0) == lax.broadcasted_iota(jnp.int32, square, 1)
    down_mine = jnp.sum(jnp.where(diagonal, mine, 0), axis=1, keepdims=True)
    down_wanted = jnp.sum(jnp.where(diagonal, wanted, 0), axis=1, keepdims=True)
    least = jnp.min(jnp.where(down_mine == mine, down_wanted, CD_DEV), axis=0, keepdims=True)
    second = (wanted > least).astype(jnp.int32)
    phase = (lax.shift_right_logical(mine, 1) - z + NZ) & 7
    dx = (lax.shift_right_logical(mine, 4) - x + NX) & 3
    dc = (mine + c) & 1
    near, far = jnp.zeros_like(mine), jnp.zeros_like(mine)
    for i, (step, core) in enumerate(LINE):
        near = jnp.where((dx == step) & (dc == core), 2 * i, near)
    for i, step in enumerate(OPPOSITE):
        far = jnp.where(dx == step, 2 * i, far)
    place = phase * 16 + jnp.where(phase == 4, far + 8 * dc, near) + second
    takes[...] = jnp.zeros(takes.shape, jnp.int32)
    takes[:, 0:NEED] = jnp.broadcast_to(place, (8, NEED))


def kernel(
    rows, total_entries, owner_list, slot_list, integ, amp, occ, vir, out, rms,
    owner_row, slot_row, owners, slots, table, takes, tab, own_tab, *refs,
):
    g0, gm1, gp1, gm2, gp2, got, sx, sd, up3, up4, down3, down4 = [refs[i * PARTS:(i + 1) * PARTS] for i in range(12)]
    (
        a0, am, ap, ao, stack, stack_low, stack_high, rows_low, rows_high, gaps, mine, sent, cols, occs, virs, sum1, sum2, load_sem, quarter_sem,
        z_send, z_recv, y_send, y_recv, x_send, d_send, f_send, relay_recv, got_recv,
        occ_sem, u_sem, s_send, s_recv,
    ) = refs[12 * PARTS:]
    own, y = lax.axis_index("own"), lax.axis_index("grp")
    x, z, c = lax.div(own, 16), lax.rem(lax.div(own, 2), 8), lax.rem(own, 2)
    half = amp.shape[1] // 2

    def at(dx=0, dy=0, dz=0, dc=0):
        nx, nz = lax.rem(x + dx + NX, NX), lax.rem(z + dz + NZ, NZ)
        return (nx * 16 + nz * 2 + lax.rem(c + dc, 2), lax.rem(y + dy + NY, NY))

    def send(src, dst, send_sem, recv_sem, device):
        copy = pltpu.make_async_remote_copy(
            src_ref=src, dst_ref=dst, send_sem=send_sem, recv_sem=recv_sem,
            device_id=device, device_id_type=MESH,
        )
        copy.start()
        return copy

    def whole(ref, sem):
        return pltpu.make_async_remote_copy(
            src_ref=ref, dst_ref=ref, send_sem=sem, recv_sem=sem,
            device_id=at(0, 0, 1, 0), device_id_type=MESH,
        )

    def arrived(ref, sem):
        whole(ref, sem).wait_recv()

    def left_here(ref, sem):
        whole(ref, sem).wait_send()

    loads = [
        pltpu.make_async_copy(
            integ.at[:, pl.ds(STARTS[h], SIZES[h]), pl.ds(pl.multiple_of(y * LANES, LANES), LANES)],
            g0[h], quarter_sem.at[h])
        for h in range(PARTS)
    ]
    loads.append(pltpu.make_async_copy(amp, a0, load_sem.at[0]))
    loads.append(pltpu.make_async_copy(occ, occs.at[0], load_sem.at[1]))
    loads.append(pltpu.make_async_copy(vir, virs, load_sem.at[2]))
    loads.append(pltpu.make_async_copy(owner_list, owner_row, load_sem.at[3]))
    loads.append(pltpu.make_async_copy(slot_list, slot_row, load_sem.at[4]))
    for copy in loads:
        copy.start()
    barrier = pltpu.get_barrier_semaphore()
    targets = [(0, 0, 1, 0), (0, 0, -1, 0)] + [(dx, 0, 0, dc) for dx, dc in LINE[1:]] + [(0, dy, 0, 0) for dy in (1, 2, 3)]
    for dx, dy, dz, dc in targets:
        pl.semaphore_signal(barrier, inc=1, device_id=at(-dx, -dy, -dz, dc), device_id_type=MESH)
    loads[0].wait()
    pl.semaphore_wait(barrier, len(targets))

    right, left = at(0, 0, 1, 0), at(0, 0, -1, 0)
    low, high = pl.ds(0, half), pl.ds(half, half)
    up, down = at(0, 1, 0, 0), at(0, -1, 0, 0)

    def pick(block, k, r, reader):
        return block[tab[reader, 2 * k + r]]

    def across(k, h, block):
        first = SHIFTS[k] % NZ * 16
        for i, (dx, dc) in enumerate(LINE[1:]):
            device = at(dx, 0, 0, dc)
            for r in range(2):
                sx[h][k, i, r] = pick(block, k, r, device[0])
            place = pl.ds(first + place_of(-dx, dc), 2)
            send(sx[h].at[k, i], got[h].at[place], x_send.at[h], got_recv.at[h], device)
        for r in range(2):
            got[h][first + r] = pick(block, k, r, own)

    def relay(k, h, block, slot, dz, dx, dc, meet, place, target):
        reader = at(dx, 0, dz, dc)[0]
        for r in range(2):
            sd[h][slot, r] = pick(block, k, r, reader)
        if (dx, dc) == (0, 0):
            send(sd[h].at[slot], got[h].at[pl.ds(target, 2)], d_send.at[h], got_recv.at[h], at(0, 0, dz, 0))
        else:
            group = 0 if (dx, dc) in GROUPS[0] else 1
            send(sd[h].at[slot], meet.at[pl.ds(place, 2)], d_send.at[h], relay_recv.at[h, group], at(dx, 0, 0, dc))

    def far(h):
        for i, (dx, dc) in enumerate(LINE):
            place, place4 = place_of(-dx, dc), place_of_opposite(-dx)
            if dc == 0:
                relay(3, h, gm2[h], 16 + dx, 2, dx, 0, up4[h], place4, FROM_UP4)
            else:
                relay(4, h, gp2[h], 20 + dx, -2, dx, 1, down4[h], place4, FROM_DOWN4)
            relay(3, h, gm2[h], i, 1, dx, dc, up3[h], place, FROM_UP3)
            relay(4, h, gp2[h], 8 + i, -1, dx, dc, down3[h], place, FROM_DOWN3)

    def onward(h, group):
        arrived(got[h].at[pl.ds(0, GROUP_ENTRIES[group])], relay_recv.at[h, group])
        lines = ((2, 6), (8, 8))[group]
        straight, crossed = ((2, 4), (6, 2))[group], ((0, 2), (2, 6))[group]
        for block, (first, count), target, device in (
            (up4[h], straight, FROM_UP4, at(0, 0, 2, 0)),
            (down4[h], crossed, FROM_DOWN4, at(0, 0, -2, 0)),
            (up3[h], lines, FROM_UP3, right),
            (down3[h], lines, FROM_DOWN3, left),
        ):
            send(block.at[pl.ds(first, count)], got[h].at[pl.ds(target + first, count)], f_send.at[h], got_recv.at[h], device)

    def first_hop(h):
        return (
            send(g0[h], gm1[h], z_send.at[0, 0, h], z_recv.at[0, 0, h], right),
            send(g0[h], gp1[h], z_send.at[1, 0, h], z_recv.at[1, 0, h], left),
        )

    def second_hop(h):
        arrived(gm1[h], z_recv.at[0, 0, h])
        onto = send(gm1[h], gm2[h], z_send.at[0, 1, h], z_recv.at[0, 1, h], right)
        arrived(gp1[h], z_recv.at[1, 0, h])
        return onto, send(gp1[h], gp2[h], z_send.at[1, 1, h], z_recv.at[1, 1, h], left)

    def come(h):
        arrived(gm2[h], z_recv.at[0, 1, h])
        arrived(gp2[h], z_recv.at[1, 1, h])

    def across_two(h):
        across(3, h, gm2[h])
        across(4, h, gp2[h])

    waiting = [*first_hop(0)]
    for h in range(1, PARTS):
        loads[h].wait()
        waiting += first_hop(h)
    first_rows = (
        send(amp.at[:, low], am.at[:, low], y_send.at[0], y_recv.at[0], up),
        send(amp.at[:, high], ap.at[:, high], y_send.at[1], y_recv.at[1], down),
    )
    for copy in loads[PARTS:]:
        copy.wait()
    for dy in (1, 2, 3):
        send(occs.at[0], occs.at[NY - dy], occ_sem.at[0], occ_sem.at[1], at(0, dy, 0, 0))
    fill_tables(own, x, z, c, owner_row, slot_row, owners, slots, table, takes)
    to_scalar = (pltpu.make_async_copy(table, tab, load_sem.at[5]), pltpu.make_async_copy(takes, own_tab, load_sem.at[6]))
    for copy in to_scalar:
        copy.start()
    for copy in to_scalar:
        copy.wait()
    across(0, 0, g0[0])
    for h in range(1, PARTS):
        across(0, h, g0[h])
        waiting += second_hop(h - 1)
        across(1, h - 1, gm1[h - 1])
        across(2, h - 1, gp1[h - 1])
    for copy in first_rows:
        copy.wait_send()
    waiting.append(send(a0.at[:, high], am.at[:, high], y_send.at[2], y_recv.at[2], up))
    waiting.append(send(a0.at[:, low], ap.at[:, low], y_send.at[3], y_recv.at[3], down))
    waiting += second_hop(PARTS - 1)
    across(1, PARTS - 1, gm1[PARTS - 1])
    across(2, PARTS - 1, gp1[PARTS - 1])
    come(0)
    far(0)
    arrived(am.at[:, low], y_recv.at[0])
    waiting.append(send(am.at[:, low], ao.at[:, low], y_send.at[4], y_recv.at[4], up))
    arrived(ap.at[:, high], y_recv.at[1])
    waiting.append(send(ap.at[:, high], ao.at[:, high], y_send.at[5], y_recv.at[5], down))
    for h in range(1, PARTS):
        onward(h - 1, 0)
        come(h)
        far(h)
        onward(h - 1, 1)
        across_two(h - 1)
    onward(PARTS - 1, 0)
    across_two(PARTS - 1)
    onward(PARTS - 1, 1)

    arrived(occs.at[pl.ds(0, 3)], occ_sem.at[1])
    diagonal = lax.broadcasted_iota(jnp.int32, (rows, rows), 0) == lax.broadcasted_iota(jnp.int32, (rows, rows), 1)
    for dy in range(NY):
        occ_rows = jnp.sum(jnp.where(diagonal, occs[dy], 0.0), axis=1, keepdims=True)
        gaps[dy] = occ_rows - virs[y]
    wide = 2 * LANES
    into = lax.broadcasted_iota(jnp.int32, (wide, wide), 1)
    middle = jnp.where(into < LANES, into + PART, into - PART)
    source = jnp.where((into >= PART) & (into < wide - PART), middle, into)
    reorder = (lax.broadcasted_iota(jnp.int32, (wide, wide), 0) == source).astype(jnp.float32).astype(jnp.bfloat16)

    def split_columns(i, block):
        for p in range(NEED // 2):
            moved = jnp.dot(block[:, p * wide:(p + 1) * wide], reorder, preferred_element_type=jnp.float32)
            moved = moved.astype(jnp.bfloat16)
            rows_low[i, :, p * LANES:(p + 1) * LANES] = moved[:, :LANES]
            rows_high[i, :, p * LANES:(p + 1) * LANES] = moved[:, LANES:]

    split_columns(0, a0)
    arrived(am.at[:, high], y_recv.at[2])
    arrived(ap.at[:, low], y_recv.at[3])
    split_columns(1, ap)
    split_columns(2, am)
    arrived(got[0].at[pl.ds(0, ARRIVING)], got_recv.at[0])
    for t in range(NEED):
        tile = got[0][own_tab[0, t]]
        stack[pl.ds(t * TILE, PART)] = tile
        stack_low[pl.ds(t * PART, PART)] = tile
    for i in range(3):
        mine[i] = jnp.dot(rows_low[i], stack_low[...], preferred_element_type=jnp.float32)
    arrived(ao.at[:, low], y_recv.at[4])
    arrived(ao.at[:, high], y_recv.at[5])
    arrived(got[1].at[pl.ds(0, ARRIVING)], got_recv.at[1])
    for t in range(NEED):
        tile = got[1][own_tab[0, t]]
        stack[pl.ds(t * TILE + PART, PART)] = tile
        stack_high[pl.ds(t * PART, PART)] = tile

    square = jnp.zeros((8, LANES), jnp.float32)
    for dy, i in ((0, 0), (1, 1), (3, 2), (2, None)):
        if i is None:
            ladder = jnp.dot(ao[...], stack[...], preferred_element_type=jnp.float32)
        else:
            ladder = mine[i] + jnp.dot(rows_high[i], stack_high[...], preferred_element_type=jnp.float32)
        update = ladder / gaps[dy]
        square = square + jnp.sum((update * update).reshape(rows // 8, 8, LANES), axis=0)
        if dy == 0:
            cols[y] = update
        else:
            sent[dy] = update

    spot = z * 2 + c
    sum1[spot] = jnp.sum(square, axis=0, keepdims=True)
    for dz in (4, 3, 5, 2, 6, 1, 7, 0):
        for dc in (1, 0):
            if (dz, dc) != (0, 0):
                send(sum1.at[spot], sum1.at[spot], s_send.at[0], s_recv.at[0], at(0, 0, dz, dc))
    for dy in (1, 2, 3):
        send(sent.at[dy], cols.at[y], u_sem.at[0], u_sem.at[1], at(0, dy, 0, 0))
    for copy in waiting:
        copy.wait_send()
    left_here(occs.at[pl.ds(0, 3)], occ_sem.at[0])
    for h in range(PARTS):
        left_here(sx[h], x_send.at[h])
        left_here(sd[h], d_send.at[h])
        left_here(got[h].at[pl.ds(0, PASSED_ON)], f_send.at[h])
    arrived(sum1.at[pl.ds(0, 15)], s_recv.at[0])
    spot = x * NY + y
    sum2[spot] = jnp.sum(sum1[...], axis=0)
    for dx in (2, 1, 3, 0):
        for dy in (2, 1, 3, 0):
            if (dx, dy) != (0, 0):
                send(sum2.at[spot], sum2.at[spot], s_send.at[1], s_recv.at[1], at(dx, dy, 0, 0))
    left_here(sum1.at[pl.ds(0, 15)], s_send.at[0])
    arrived(cols.at[pl.ds(0, 3)], u_sem.at[1])
    stores = []
    for k in range(NY):
        stores.append(pltpu.make_async_copy(cols.at[k], out.at[:, pl.ds(k * LANES, LANES)], load_sem.at[k]))
        stores[k].start()
    left_here(cols.at[pl.ds(0, 3)], u_sem.at[0])
    arrived(sum2.at[pl.ds(0, 15)], s_recv.at[1])
    everything = jnp.sum(jnp.sum(sum2[...], axis=0), axis=1, keepdims=True)
    rms[...] = jnp.sqrt(everything / total_entries)
    for copy in stores:
        copy.wait()
    left_here(sum2.at[pl.ds(0, 15)], s_send.at[1])


def per_device(amplitudes, integrals, task_owner, task_slot, occ_pair, vir_pair):
    rows, depth = amplitudes.shape
    columns = integrals.shape[1]
    bf16, f32, i32 = jnp.bfloat16, jnp.float32, jnp.int32
    dma = pltpu.SemaphoreType.DMA

    def body(*refs):
        kernel(rows, float(rows * OWNERS * NY * columns), *refs)

    def parts(*lead):
        return [pltpu.VMEM((*lead, size, LANES), bf16) for size in SIZES]

    anywhere, vmem = pl.BlockSpec(memory_space=pltpu.HBM), pl.BlockSpec(memory_space=pltpu.VMEM)
    update, rms = pl.pallas_call(
        body,
        out_shape=(
            jax.ShapeDtypeStruct((rows, columns), f32),
            jax.ShapeDtypeStruct((1, 1), f32),
        ),
        in_specs=[anywhere] * 6,
        out_specs=(anywhere, vmem),
        scratch_shapes=[
            *[pltpu.VMEM((1, OWNERS * NEED), i32)] * 2,
            *[pltpu.VMEM((OWNERS, NEED), i32)] * 2,
            pltpu.VMEM((OWNERS, LANES), i32),
            pltpu.VMEM((8, LANES), i32),
            pltpu.SMEM((OWNERS, LANES), i32),
            pltpu.SMEM((8, LANES), i32),
            *parts(CD_DEV), *parts(CD_DEV), *parts(CD_DEV), *parts(CD_DEV), *parts(CD_DEV),
            *parts(2 * OWNERS), *parts(5, 7, 2), *parts(24, 2),
            *parts(16), *parts(8), *parts(16), *parts(8),
            *[pltpu.VMEM((rows, depth), bf16)] * 4,
            pltpu.VMEM((depth, LANES), bf16),
            *[pltpu.VMEM((depth // 2, LANES), bf16)] * 2,
            *[pltpu.VMEM((3, rows, depth // 2), bf16)] * 2,
            *[pltpu.VMEM((NY, rows, LANES), f32)] * 4,
            pltpu.VMEM((NY, 1, rows), f32),
            pltpu.VMEM((NY, 1, LANES), f32),
            *[pltpu.VMEM((16, 1, LANES), f32)] * 2,
            dma((7,)), dma((PARTS,)),
            dma((2, 2, PARTS)), dma((2, 2, PARTS)),
            dma((6,)), dma((6,)),
            dma((PARTS,)), dma((PARTS,)), dma((PARTS,)), dma((PARTS, 2)), dma((PARTS,)),
            dma((2,)), dma((2,)), dma((2,)), dma((2,)),
        ],
        compiler_params=pltpu.CompilerParams(
            collective_id=0, has_side_effects=True, vmem_limit_bytes=56 << 20
        ),
        cost_estimate=pl.CostEstimate(
            flops=2 * rows * depth * columns, bytes_accessed=8 << 20, transcendentals=0
        ),
        name="ladder",
    )(
        task_owner.T,
        task_slot.T,
        integrals.reshape(CD_DEV, TILE, columns),
        amplitudes,
        occ_pair.reshape(1, rows),
        vir_pair.reshape(NY, 1, LANES),
    )
    return update, rms[0, 0]


def solution(mesh):
    placed = (P(("own", "grp"), None), P("own", None), P(), P(), P(("own", "grp")), P())
    return jax.shard_map(
        per_device,
        mesh=mesh,
        in_specs=placed,
        out_specs=(P(("own", "grp"), None), P()),
        check_vma=False,
    )
```

```python
import jax
import jax.numpy as jnp
from jax import lax
from jax.experimental import pallas as pl
from jax.experimental.pallas import tpu as pltpu
from jax.sharding import PartitionSpec as P

MESH = pl.DeviceIdType.MESH
TILE = 128
PART = 64
SIZES = (PART, PART)
PARTS = len(SIZES)
STARTS = tuple(sum(SIZES[:h]) for h in range(PARTS))
CD_DEV = 24
NEED = 44
OWNERS = 64
NX, NY, NZ = 4, 4, 8
LANES = 128
SHIFTS = (0, -1, 1, -2, 2)
LINE = ((0, 0), (0, 1), (1, 0), (3, 0), (1, 1), (3, 1), (2, 0), (2, 1))
OPPOSITE = (0, 1, 3, 2)
GROUPS = (LINE[1:4], LINE[4:])
GROUP_ENTRIES = (18, 24)
FROM_UP3, FROM_DOWN3, FROM_UP4, FROM_DOWN4, ALL_FAR = 80, 48, 64, 72, 48
ARRIVING = 5 * 14 + ALL_FAR
PASSED_ON = 42


def place_of(dx, dc):
    return LINE.index((dx % NX, dc)) * 2


def place_of_opposite(dx):
    return OPPOSITE.index(dx % NX) * 2


def fill_tables(own, x, z, c, owner_row, slot_row, owners, slots, table, takes):
    for reader in range(OWNERS):
        listed = slice(reader * NEED, (reader + 1) * NEED)
        owners[reader:reader + 1, :] = owner_row[0:1, listed]
        slots[reader:reader + 1, :] = slot_row[0:1, listed]
    lane = lax.broadcasted_iota(jnp.int32, (OWNERS, LANES), 1)
    filled = jnp.zeros((OWNERS, LANES), jnp.int32)
    for k, shift in enumerate(SHIFTS):
        source = x * 16 + lax.rem(z + shift + NZ, NZ) * 2 + c
        same = owners[...] == source
        first = jnp.min(jnp.where(same, slots[...], CD_DEV - 1), axis=1, keepdims=True)
        last = jnp.max(jnp.where(same, slots[...], 0), axis=1, keepdims=True)
        filled = jnp.where(lane == 2 * k, first, filled)
        filled = jnp.where(lane == 2 * k + 1, last, filled)
    table[...] = filled
    mine, wanted = owners[pl.ds(own, 1), :], slots[pl.ds(own, 1), :]
    square = (NEED, NEED)
    diagonal = lax.broadcasted_iota(jnp.int32, square, 0) == lax.broadcasted_iota(jnp.int32, square, 1)
    down_mine = jnp.sum(jnp.where(diagonal, mine, 0), axis=1, keepdims=True)
    down_wanted = jnp.sum(jnp.where(diagonal, wanted, 0), axis=1, keepdims=True)
    least = jnp.min(jnp.where(down_mine == mine, down_wanted, CD_DEV), axis=0, keepdims=True)
    second = (wanted > least).astype(jnp.int32)
    phase = (lax.shift_right_logical(mine, 1) - z + NZ) & 7
    dx = (lax.shift_right_logical(mine, 4) - x + NX) & 3
    dc = (mine + c) & 1
    near, far = jnp.zeros_like(mine), jnp.zeros_like(mine)
    for i, (step, core) in enumerate(LINE):
        near = jnp.where((dx == step) & (dc == core), 2 * i, near)
    for i, step in enumerate(OPPOSITE):
        far = jnp.where(dx == step, 2 * i, far)
    place = phase * 16 + jnp.where(phase == 4, far + 8 * dc, near) + second
    takes[...] = jnp.zeros(takes.shape, jnp.int32)
    takes[:, 0:NEED] = jnp.broadcast_to(place, (8, NEED))


def kernel(
    rows, total_entries, owner_list, slot_list, integ, amp, occ, vir, out, rms,
    owner_row, slot_row, owners, slots, table, takes, tab, own_tab, *refs,
):
    g0, gm1, gp1, gm2, gp2, got, sx, sd, up3, up4, down3, down4 = [refs[i * PARTS:(i + 1) * PARTS] for i in range(12)]
    (
        a0, am, ap, ao, stack, stack_low, stack_high, rows_low, rows_high, gaps, mine, sent, cols, occs, virs, sum1, sum2, load_sem, quarter_sem,
        z_send, z_recv, y_send, y_recv, x_send, d_send, f_send, relay_recv, got_recv,
        occ_sem, u_sem, s_send, s_recv,
    ) = refs[12 * PARTS:]
    own, y = lax.axis_index("own"), lax.axis_index("grp")
    x, z, c = lax.div(own, 16), lax.rem(lax.div(own, 2), 8), lax.rem(own, 2)
    half = amp.shape[1] // 2

    def at(dx=0, dy=0, dz=0, dc=0):
        nx, nz = lax.rem(x + dx + NX, NX), lax.rem(z + dz + NZ, NZ)
        return (nx * 16 + nz * 2 + lax.rem(c + dc, 2), lax.rem(y + dy + NY, NY))

    def send(src, dst, send_sem, recv_sem, device):
        copy = pltpu.make_async_remote_copy(
            src_ref=src, dst_ref=dst, send_sem=send_sem, recv_sem=recv_sem,
            device_id=device, device_id_type=MESH,
        )
        copy.start()
        return copy

    def whole(ref, sem):
        return pltpu.make_async_remote_copy(
            src_ref=ref, dst_ref=ref, send_sem=sem, recv_sem=sem,
            device_id=at(0, 0, 1, 0), device_id_type=MESH,
        )

    def arrived(ref, sem):
        whole(ref, sem).wait_recv()

    def left_here(ref, sem):
        whole(ref, sem).wait_send()

    loads = [
        pltpu.make_async_copy(
            integ.at[:, pl.ds(STARTS[h], SIZES[h]), pl.ds(pl.multiple_of(y * LANES, LANES), LANES)],
            g0[h], quarter_sem.at[h])
        for h in range(PARTS)
    ]
    loads.append(pltpu.make_async_copy(amp, a0, load_sem.at[0]))
    loads.append(pltpu.make_async_copy(occ, occs.at[0], load_sem.at[1]))
    loads.append(pltpu.make_async_copy(vir, virs, load_sem.at[2]))
    loads.append(pltpu.make_async_copy(owner_list, owner_row, load_sem.at[3]))
    loads.append(pltpu.make_async_copy(slot_list, slot_row, load_sem.at[4]))
    for copy in loads:
        copy.start()
    barrier = pltpu.get_barrier_semaphore()
    targets = [(0, 0, 1, 0), (0, 0, -1, 0)] + [(dx, 0, 0, dc) for dx, dc in LINE[1:]] + [(0, dy, 0, 0) for dy in (1, 2, 3)]
    for dx, dy, dz, dc in targets:
        pl.semaphore_signal(barrier, inc=1, device_id=at(-dx, -dy, -dz, dc), device_id_type=MESH)
    loads[0].wait()
    pl.semaphore_wait(barrier, len(targets))

    right, left = at(0, 0, 1, 0), at(0, 0, -1, 0)
    low, high = pl.ds(0, half), pl.ds(half, half)
    up, down = at(0, 1, 0, 0), at(0, -1, 0, 0)

    def pick(block, k, r, reader):
        return block[tab[reader, 2 * k + r]]

    def across(k, h, block):
        first = SHIFTS[k] % NZ * 16
        for i, (dx, dc) in enumerate(LINE[1:]):
            device = at(dx, 0, 0, dc)
            for r in range(2):
                sx[h][k, i, r] = pick(block, k, r, device[0])
            place = pl.ds(first + place_of(-dx, dc), 2)
            send(sx[h].at[k, i], got[h].at[place], x_send.at[h], got_recv.at[h], device)
        for r in range(2):
            got[h][first + r] = pick(block, k, r, own)

    def relay(k, h, block, slot, dz, dx, dc, meet, place, target):
        reader = at(dx, 0, dz, dc)[0]
        for r in range(2):
            sd[h][slot, r] = pick(block, k, r, reader)
        if (dx, dc) == (0, 0):
            send(sd[h].at[slot], got[h].at[pl.ds(target, 2)], d_send.at[h], got_recv.at[h], at(0, 0, dz, 0))
        else:
            group = 0 if (dx, dc) in GROUPS[0] else 1
            send(sd[h].at[slot], meet.at[pl.ds(place, 2)], d_send.at[h], relay_recv.at[h, group], at(dx, 0, 0, dc))

    def far(h):
        for i, (dx, dc) in enumerate(LINE):
            place, place4 = place_of(-dx, dc), place_of_opposite(-dx)
            if dc == 0:
                relay(3, h, gm2[h], 16 + dx, 2, dx, 0, up4[h], place4, FROM_UP4)
            else:
                relay(4, h, gp2[h], 20 + dx, -2, dx, 1, down4[h], place4, FROM_DOWN4)
            relay(3, h, gm2[h], i, 1, dx, dc, up3[h], place, FROM_UP3)
            relay(4, h, gp2[h], 8 + i, -1, dx, dc, down3[h], place, FROM_DOWN3)

    def onward(h, group):
        arrived(got[h].at[pl.ds(0, GROUP_ENTRIES[group])], relay_recv.at[h, group])
        lines = ((2, 6), (8, 8))[group]
        straight, crossed = ((2, 4), (6, 2))[group], ((0, 2), (2, 6))[group]
        for block, (first, count), target, device in (
            (up4[h], straight, FROM_UP4, at(0, 0, 2, 0)),
            (down4[h], crossed, FROM_DOWN4, at(0, 0, -2, 0)),
            (up3[h], lines, FROM_UP3, right),
            (down3[h], lines, FROM_DOWN3, left),
        ):
            send(block.at[pl.ds(first, count)], got[h].at[pl.ds(target + first, count)], f_send.at[h], got_recv.at[h], device)

    def first_hop(h):
        return (
            send(g0[h], gm1[h], z_send.at[0], z_recv.at[0, h], right),
            send(g0[h], gp1[h], z_send.at[0], z_recv.at[0, h], left),
        )

    def second_hop(h):
        arrived(got[h].at[pl.ds(0, 2 * CD_DEV)], z_recv.at[0, h])
        onto = send(gm1[h], gm2[h], z_send.at[1], z_recv.at[1, h], right)
        return onto, send(gp1[h], gp2[h], z_send.at[1], z_recv.at[1, h], left)

    def come(h):
        arrived(got[h].at[pl.ds(0, 2 * CD_DEV)], z_recv.at[1, h])

    def across_two(h):
        across(3, h, gm2[h])
        across(4, h, gp2[h])

    first_hop(0)
    for h in range(1, PARTS):
        loads[h].wait()
        first_hop(h)
    send(amp.at[:, low], am.at[:, low], y_send.at[0], y_recv.at[0], up)
    send(amp.at[:, high], ap.at[:, high], y_send.at[0], y_recv.at[0], down)
    for copy in loads[PARTS:]:
        copy.wait()
    for dy in (1, 2, 3):
        send(occs.at[0], occs.at[NY - dy], occ_sem.at[0], occ_sem.at[1], at(0, dy, 0, 0))
    fill_tables(own, x, z, c, owner_row, slot_row, owners, slots, table, takes)
    to_scalar = (pltpu.make_async_copy(table, tab, load_sem.at[5]), pltpu.make_async_copy(takes, own_tab, load_sem.at[6]))
    for copy in to_scalar:
        copy.start()
    for copy in to_scalar:
        copy.wait()
    across(0, 0, g0[0])
    for h in range(1, PARTS):
        across(0, h, g0[h])
        second_hop(h - 1)
        across(1, h - 1, gm1[h - 1])
        across(2, h - 1, gp1[h - 1])
    left_here(a0, y_send.at[0])
    send(a0.at[:, high], am.at[:, high], y_send.at[1], y_recv.at[1], up)
    send(a0.at[:, low], ap.at[:, low], y_send.at[1], y_recv.at[1], down)
    second_hop(PARTS - 1)
    across(1, PARTS - 1, gm1[PARTS - 1])
    across(2, PARTS - 1, gp1[PARTS - 1])
    come(0)
    far(0)
    arrived(a0, y_recv.at[0])
    send(am.at[:, low], ao.at[:, low], y_send.at[2], y_recv.at[2], up)
    send(ap.at[:, high], ao.at[:, high], y_send.at[2], y_recv.at[2], down)
    for h in range(1, PARTS):
        onward(h - 1, 0)
        come(h)
        far(h)
        onward(h - 1, 1)
        across_two(h - 1)
    onward(PARTS - 1, 0)
    across_two(PARTS - 1)
    onward(PARTS - 1, 1)

    arrived(occs.at[pl.ds(0, 3)], occ_sem.at[1])
    diagonal = lax.broadcasted_iota(jnp.int32, (rows, rows), 0) == lax.broadcasted_iota(jnp.int32, (rows, rows), 1)
    for dy in range(NY):
        occ_rows = jnp.sum(jnp.where(diagonal, occs[dy], 0.0), axis=1, keepdims=True)
        gaps[dy] = occ_rows - virs[y]
    wide = 2 * LANES
    into = lax.broadcasted_iota(jnp.int32, (wide, wide), 1)
    middle = jnp.where(into < LANES, into + PART, into - PART)
    source = jnp.where((into >= PART) & (into < wide - PART), middle, into)
    reorder = (lax.broadcasted_iota(jnp.int32, (wide, wide), 0) == source).astype(jnp.float32).astype(jnp.bfloat16)

    def split_columns(i, block):
        for p in range(NEED // 2):
            moved = jnp.dot(block[:, p * wide:(p + 1) * wide], reorder, preferred_element_type=jnp.float32)
            moved = moved.astype(jnp.bfloat16)
            rows_low[i, :, p * LANES:(p + 1) * LANES] = moved[:, :LANES]
            rows_high[i, :, p * LANES:(p + 1) * LANES] = moved[:, LANES:]

    split_columns(0, a0)
    arrived(a0, y_recv.at[1])
    split_columns(1, ap)
    split_columns(2, am)
    arrived(got[0].at[pl.ds(0, ARRIVING)], got_recv.at[0])
    for t in range(NEED):
        tile = got[0][own_tab[0, t]]
        stack[pl.ds(t * TILE, PART)] = tile
        stack_low[pl.ds(t * PART, PART)] = tile
    for i in range(3):
        mine[i] = jnp.dot(rows_low[i], stack_low[...], preferred_element_type=jnp.float32)
    arrived(ao, y_recv.at[2])
    arrived(got[1].at[pl.ds(0, ARRIVING)], got_recv.at[1])
    for t in range(NEED):
        tile = got[1][own_tab[0, t]]
        stack[pl.ds(t * TILE + PART, PART)] = tile
        stack_high[pl.ds(t * PART, PART)] = tile

    square = jnp.zeros((8, LANES), jnp.float32)
    for dy, i in ((0, 0), (1, 1), (3, 2), (2, None)):
        if i is None:
            ladder = jnp.dot(ao[...], stack[...], preferred_element_type=jnp.float32)
        else:
            ladder = mine[i] + jnp.dot(rows_high[i], stack_high[...], preferred_element_type=jnp.float32)
        update = ladder / gaps[dy]
        square = square + jnp.sum((update * update).reshape(rows // 8, 8, LANES), axis=0)
        if dy == 0:
            cols[y] = update
        else:
            sent[dy] = update

    spot = z * 2 + c
    sum1[spot] = jnp.sum(square, axis=0, keepdims=True)
    for dz in (4, 3, 5, 2, 6, 1, 7, 0):
        for dc in (1, 0):
            if (dz, dc) != (0, 0):
                send(sum1.at[spot], sum1.at[spot], s_send.at[0], s_recv.at[0], at(0, 0, dz, dc))
    for dy in (1, 2, 3):
        send(sent.at[dy], cols.at[y], u_sem.at[0], u_sem.at[1], at(0, dy, 0, 0))
    left_here(a0, y_send.at[1])
    left_here(ao, y_send.at[2])
    left_here(occs.at[pl.ds(0, 3)], occ_sem.at[0])
    for hop in range(2):
        left_here(got[0].at[pl.ds(0, 4 * CD_DEV)], z_send.at[hop])
    for h in range(PARTS):
        left_here(sx[h], x_send.at[h])
        left_here(sd[h], d_send.at[h])
        left_here(got[h].at[pl.ds(0, PASSED_ON)], f_send.at[h])
    arrived(sum1.at[pl.ds(0, 15)], s_recv.at[0])
    spot = x * NY + y
    sum2[spot] = jnp.sum(sum1[...], axis=0)
    for dx in (2, 1, 3, 0):
        for dy in (2, 1, 3, 0):
            if (dx, dy) != (0, 0):
                send(sum2.at[spot], sum2.at[spot], s_send.at[1], s_recv.at[1], at(dx, dy, 0, 0))
    left_here(sum1.at[pl.ds(0, 15)], s_send.at[0])
    arrived(cols.at[pl.ds(0, 3)], u_sem.at[1])
    stores = []
    for k in range(NY):
        stores.append(pltpu.make_async_copy(cols.at[k], out.at[:, pl.ds(k * LANES, LANES)], load_sem.at[k]))
        stores[k].start()
    left_here(cols.at[pl.ds(0, 3)], u_sem.at[0])
    arrived(sum2.at[pl.ds(0, 15)], s_recv.at[1])
    everything = jnp.sum(jnp.sum(sum2[...], axis=0), axis=1, keepdims=True)
    rms[...] = jnp.sqrt(everything / total_entries)
    for copy in stores:
        copy.wait()
    left_here(sum2.at[pl.ds(0, 15)], s_send.at[1])


def per_device(amplitudes, integrals, task_owner, task_slot, occ_pair, vir_pair):
    rows, depth = amplitudes.shape
    columns = integrals.shape[1]
    bf16, f32, i32 = jnp.bfloat16, jnp.float32, jnp.int32
    dma = pltpu.SemaphoreType.DMA

    def body(*refs):
        kernel(rows, float(rows * OWNERS * NY * columns), *refs)

    def parts(*lead):
        return [pltpu.VMEM((*lead, size, LANES), bf16) for size in SIZES]

    anywhere, vmem = pl.BlockSpec(memory_space=pltpu.HBM), pl.BlockSpec(memory_space=pltpu.VMEM)
    update, rms = pl.pallas_call(
        body,
        out_shape=(
            jax.ShapeDtypeStruct((rows, columns), f32),
            jax.ShapeDtypeStruct((1, 1), f32),
        ),
        in_specs=[anywhere] * 6,
        out_specs=(anywhere, vmem),
        scratch_shapes=[
            *[pltpu.VMEM((1, OWNERS * NEED), i32)] * 2,
            *[pltpu.VMEM((OWNERS, NEED), i32)] * 2,
            pltpu.VMEM((OWNERS, LANES), i32),
            pltpu.VMEM((8, LANES), i32),
            pltpu.SMEM((OWNERS, LANES), i32),
            pltpu.SMEM((8, LANES), i32),
            *parts(CD_DEV), *parts(CD_DEV), *parts(CD_DEV), *parts(CD_DEV), *parts(CD_DEV),
            *parts(2 * OWNERS), *parts(5, 7, 2), *parts(24, 2),
            *parts(16), *parts(8), *parts(16), *parts(8),
            *[pltpu.VMEM((rows, depth), bf16)] * 4,
            pltpu.VMEM((depth, LANES), bf16),
            *[pltpu.VMEM((depth // 2, LANES), bf16)] * 2,
            *[pltpu.VMEM((3, rows, depth // 2), bf16)] * 2,
            *[pltpu.VMEM((NY, rows, LANES), f32)] * 4,
            pltpu.VMEM((NY, 1, rows), f32),
            pltpu.VMEM((NY, 1, LANES), f32),
            *[pltpu.VMEM((16, 1, LANES), f32)] * 2,
            dma((7,)), dma((PARTS,)),
            dma((2,)), dma((2, PARTS)),
            dma((3,)), dma((3,)),
            dma((PARTS,)), dma((PARTS,)), dma((PARTS,)), dma((PARTS, 2)), dma((PARTS,)),
            dma((2,)), dma((2,)), dma((2,)), dma((2,)),
        ],
        compiler_params=pltpu.CompilerParams(
            collective_id=0, has_side_effects=True, vmem_limit_bytes=56 << 20
        ),
        cost_estimate=pl.CostEstimate(
            flops=2 * rows * depth * columns, bytes_accessed=8 << 20, transcendentals=0
        ),
        name="ladder",
    )(
        task_owner.T,
        task_slot.T,
        integrals.reshape(CD_DEV, TILE, columns),
        amplitudes,
        occ_pair.reshape(1, rows),
        vir_pair.reshape(NY, 1, LANES),
    )
    return update, rms[0, 0]


def solution(mesh):
    placed = (P(("own", "grp"), None), P("own", None), P(), P(), P(("own", "grp")), P())
    return jax.shard_map(
        per_device,
        mesh=mesh,
        in_specs=placed,
        out_specs=(P(("own", "grp"), None), P()),
        check_vma=False,
    )
```

```python
import jax
import jax.numpy as jnp
from jax import lax
from jax.experimental import pallas as pl
from jax.experimental.pallas import tpu as pltpu
from jax.sharding import PartitionSpec as P

MESH = pl.DeviceIdType.MESH
TILE = 128
PART = 64
SIZES = (PART, PART)
PARTS = len(SIZES)
STARTS = tuple(sum(SIZES[:h]) for h in range(PARTS))
CD_DEV = 24
NEED = 44
OWNERS = 64
NX, NY, NZ = 4, 4, 8
LANES = 128
SHIFTS = (0, -1, 1, -2, 2)
LINE = ((0, 0), (0, 1), (1, 0), (3, 0), (1, 1), (3, 1), (2, 0), (2, 1))
OPPOSITE = (0, 1, 3, 2)
GROUPS = (LINE[1:4], LINE[4:])
GROUP_ENTRIES = (18, 24)
FROM_UP3, FROM_DOWN3, FROM_UP4, FROM_DOWN4, ALL_FAR = 80, 48, 64, 72, 48
ARRIVING = 5 * 14 + ALL_FAR
PASSED_ON = 42


def place_of(dx, dc):
    return LINE.index((dx % NX, dc)) * 2


def place_of_opposite(dx):
    return OPPOSITE.index(dx % NX) * 2


def fill_tables(own, x, z, c, owner_row, slot_row, owners, slots, table, takes):
    for reader in range(OWNERS):
        listed = slice(reader * NEED, (reader + 1) * NEED)
        owners[reader:reader + 1, :] = owner_row[0:1, listed]
        slots[reader:reader + 1, :] = slot_row[0:1, listed]
    lane = lax.broadcasted_iota(jnp.int32, (OWNERS, LANES), 1)
    filled = jnp.zeros((OWNERS, LANES), jnp.int32)
    for k, shift in enumerate(SHIFTS):
        source = x * 16 + lax.rem(z + shift + NZ, NZ) * 2 + c
        same = owners[...] == source
        first = jnp.min(jnp.where(same, slots[...], CD_DEV - 1), axis=1, keepdims=True)
        last = jnp.max(jnp.where(same, slots[...], 0), axis=1, keepdims=True)
        filled = jnp.where(lane == 2 * k, first, filled)
        filled = jnp.where(lane == 2 * k + 1, last, filled)
    table[...] = filled
    mine, wanted = owners[pl.ds(own, 1), :], slots[pl.ds(own, 1), :]
    square = (NEED, NEED)
    diagonal = lax.broadcasted_iota(jnp.int32, square, 0) == lax.broadcasted_iota(jnp.int32, square, 1)
    down_mine = jnp.sum(jnp.where(diagonal, mine, 0), axis=1, keepdims=True)
    down_wanted = jnp.sum(jnp.where(diagonal, wanted, 0), axis=1, keepdims=True)
    least = jnp.min(jnp.where(down_mine == mine, down_wanted, CD_DEV), axis=0, keepdims=True)
    second = (wanted > least).astype(jnp.int32)
    phase = (lax.shift_right_logical(mine, 1) - z + NZ) & 7
    dx = (lax.shift_right_logical(mine, 4) - x + NX) & 3
    dc = (mine + c) & 1
    near, far = jnp.zeros_like(mine), jnp.zeros_like(mine)
    for i, (step, core) in enumerate(LINE):
        near = jnp.where((dx == step) & (dc == core), 2 * i, near)
    for i, step in enumerate(OPPOSITE):
        far = jnp.where(dx == step, 2 * i, far)
    place = phase * 16 + jnp.where(phase == 4, far + 8 * dc, near) + second
    takes[...] = jnp.zeros(takes.shape, jnp.int32)
    takes[:, 0:NEED] = jnp.broadcast_to(place, (8, NEED))


def kernel(
    rows, total_entries, owner_list, slot_list, integ, amp, occ, vir, out, rms,
    owner_row, slot_row, owners, slots, table, takes, tab, own_tab, *refs,
):
    g0, gm1, gp1, gm2, gp2, got, sx, sd, up3, up4, down3, down4 = [refs[i * PARTS:(i + 1) * PARTS] for i in range(12)]
    (
        a0, am, ap, ao, stack_low, stack_high, rows_low, rows_high, gaps, mine, sent, cols, occs, virs, sum1, sum2, load_sem, quarter_sem,
        z_send, z_recv, y_send, y_recv, x_send, d_send, f_send, relay_recv, got_recv,
        occ_sem, u_sem, s_send, s_recv,
    ) = refs[12 * PARTS:]
    own, y = lax.axis_index("own"), lax.axis_index("grp")
    x, z, c = lax.div(own, 16), lax.rem(lax.div(own, 2), 8), lax.rem(own, 2)
    half = amp.shape[1] // 2

    def at(dx=0, dy=0, dz=0, dc=0):
        nx, nz = lax.rem(x + dx + NX, NX), lax.rem(z + dz + NZ, NZ)
        return (nx * 16 + nz * 2 + lax.rem(c + dc, 2), lax.rem(y + dy + NY, NY))

    def send(src, dst, send_sem, recv_sem, device):
        copy = pltpu.make_async_remote_copy(
            src_ref=src, dst_ref=dst, send_sem=send_sem, recv_sem=recv_sem,
            device_id=device, device_id_type=MESH,
        )
        copy.start()
        return copy

    def whole(ref, sem):
        return pltpu.make_async_remote_copy(
            src_ref=ref, dst_ref=ref, send_sem=sem, recv_sem=sem,
            device_id=at(0, 0, 1, 0), device_id_type=MESH,
        )

    def arrived(ref, sem):
        whole(ref, sem).wait_recv()

    def left_here(ref, sem):
        whole(ref, sem).wait_send()

    loads = [
        pltpu.make_async_copy(
            integ.at[:, pl.ds(STARTS[h], SIZES[h]), pl.ds(pl.multiple_of(y * LANES, LANES), LANES)],
            g0[h], quarter_sem.at[h])
        for h in range(PARTS)
    ]
    loads.append(pltpu.make_async_copy(amp, a0, load_sem.at[0]))
    loads.append(pltpu.make_async_copy(occ, occs.at[0], load_sem.at[1]))
    loads.append(pltpu.make_async_copy(vir, virs, load_sem.at[2]))
    loads.append(pltpu.make_async_copy(owner_list, owner_row, load_sem.at[3]))
    loads.append(pltpu.make_async_copy(slot_list, slot_row, load_sem.at[4]))
    for copy in loads:
        copy.start()
    barrier = pltpu.get_barrier_semaphore()
    targets = [(0, 0, 1, 0), (0, 0, -1, 0)] + [(dx, 0, 0, dc) for dx, dc in LINE[1:]] + [(0, dy, 0, 0) for dy in (1, 2, 3)]
    for dx, dy, dz, dc in targets:
        pl.semaphore_signal(barrier, inc=1, device_id=at(-dx, -dy, -dz, dc), device_id_type=MESH)
    loads[0].wait()
    pl.semaphore_wait(barrier, len(targets))

    right, left = at(0, 0, 1, 0), at(0, 0, -1, 0)
    low, high = pl.ds(0, half), pl.ds(half, half)
    up, down = at(0, 1, 0, 0), at(0, -1, 0, 0)

    def pick(block, k, r, reader):
        return block[tab[reader, 2 * k + r]]

    def across(k, h, block):
        first = SHIFTS[k] % NZ * 16
        for i, (dx, dc) in enumerate(LINE[1:]):
            device = at(dx, 0, 0, dc)
            for r in range(2):
                sx[h][k, i, r] = pick(block, k, r, device[0])
            place = pl.ds(first + place_of(-dx, dc), 2)
            send(sx[h].at[k, i], got[h].at[place], x_send.at[h], got_recv.at[h], device)
        for r in range(2):
            got[h][first + r] = pick(block, k, r, own)

    def relay(k, h, block, slot, dz, dx, dc, meet, place, target):
        reader = at(dx, 0, dz, dc)[0]
        for r in range(2):
            sd[h][slot, r] = pick(block, k, r, reader)
        if (dx, dc) == (0, 0):
            send(sd[h].at[slot], got[h].at[pl.ds(target, 2)], d_send.at[h], got_recv.at[h], at(0, 0, dz, 0))
        else:
            group = 0 if (dx, dc) in GROUPS[0] else 1
            send(sd[h].at[slot], meet.at[pl.ds(place, 2)], d_send.at[h], relay_recv.at[h, group], at(dx, 0, 0, dc))

    def far(h):
        for i, (dx, dc) in enumerate(LINE):
            place, place4 = place_of(-dx, dc), place_of_opposite(-dx)
            if dc == 0:
                relay(3, h, gm2[h], 16 + dx, 2, dx, 0, up4[h], place4, FROM_UP4)
            else:
                relay(4, h, gp2[h], 20 + dx, -2, dx, 1, down4[h], place4, FROM_DOWN4)
            relay(3, h, gm2[h], i, 1, dx, dc, up3[h], place, FROM_UP3)
            relay(4, h, gp2[h], 8 + i, -1, dx, dc, down3[h], place, FROM_DOWN3)

    def onward(h, group):
        arrived(got[h].at[pl.ds(0, GROUP_ENTRIES[group])], relay_recv.at[h, group])
        lines = ((2, 6), (8, 8))[group]
        straight, crossed = ((2, 4), (6, 2))[group], ((0, 2), (2, 6))[group]
        for block, (first, count), target, device in (
            (up4[h], straight, FROM_UP4, at(0, 0, 2, 0)),
            (down4[h], crossed, FROM_DOWN4, at(0, 0, -2, 0)),
            (up3[h], lines, FROM_UP3, right),
            (down3[h], lines, FROM_DOWN3, left),
        ):
            send(block.at[pl.ds(first, count)], got[h].at[pl.ds(target + first, count)], f_send.at[h], got_recv.at[h], device)

    def first_hop(h):
        return (
            send(g0[h], gm1[h], z_send.at[0], z_recv.at[0, h], right),
            send(g0[h], gp1[h], z_send.at[0], z_recv.at[0, h], left),
        )

    def second_hop(h):
        arrived(got[h].at[pl.ds(0, 2 * CD_DEV)], z_recv.at[0, h])
        onto = send(gm1[h], gm2[h], z_send.at[1], z_recv.at[1, h], right)
        return onto, send(gp1[h], gp2[h], z_send.at[1], z_recv.at[1, h], left)

    def come(h):
        arrived(got[h].at[pl.ds(0, 2 * CD_DEV)], z_recv.at[1, h])

    def across_two(h):
        across(3, h, gm2[h])
        across(4, h, gp2[h])

    first_hop(0)
    for h in range(1, PARTS):
        loads[h].wait()
        first_hop(h)
    send(amp.at[:, low], am.at[:, low], y_send.at[0], y_recv.at[0], up)
    send(amp.at[:, high], ap.at[:, high], y_send.at[0], y_recv.at[0], down)
    for copy in loads[PARTS:]:
        copy.wait()
    for dy in (1, 2, 3):
        send(occs.at[0], occs.at[NY - dy], occ_sem.at[0], occ_sem.at[1], at(0, dy, 0, 0))
    fill_tables(own, x, z, c, owner_row, slot_row, owners, slots, table, takes)
    to_scalar = (pltpu.make_async_copy(table, tab, load_sem.at[5]), pltpu.make_async_copy(takes, own_tab, load_sem.at[6]))
    for copy in to_scalar:
        copy.start()
    for copy in to_scalar:
        copy.wait()
    across(0, 0, g0[0])
    for h in range(1, PARTS):
        across(0, h, g0[h])
        second_hop(h - 1)
        across(1, h - 1, gm1[h - 1])
        across(2, h - 1, gp1[h - 1])
    left_here(a0, y_send.at[0])
    send(a0.at[:, high], am.at[:, high], y_send.at[1], y_recv.at[1], up)
    send(a0.at[:, low], ap.at[:, low], y_send.at[1], y_recv.at[1], down)
    second_hop(PARTS - 1)
    across(1, PARTS - 1, gm1[PARTS - 1])
    across(2, PARTS - 1, gp1[PARTS - 1])
    come(0)
    far(0)
    arrived(a0, y_recv.at[0])
    send(am.at[:, low], ao.at[:, low], y_send.at[2], y_recv.at[2], up)
    send(ap.at[:, high], ao.at[:, high], y_send.at[2], y_recv.at[2], down)
    for h in range(1, PARTS):
        onward(h - 1, 0)
        come(h)
        far(h)
        onward(h - 1, 1)
        across_two(h - 1)
    onward(PARTS - 1, 0)
    across_two(PARTS - 1)
    onward(PARTS - 1, 1)

    arrived(occs.at[pl.ds(0, 3)], occ_sem.at[1])
    diagonal = lax.broadcasted_iota(jnp.int32, (rows, rows), 0) == lax.broadcasted_iota(jnp.int32, (rows, rows), 1)
    for dy in range(NY):
        occ_rows = jnp.sum(jnp.where(diagonal, occs[dy], 0.0), axis=1, keepdims=True)
        gaps[dy] = occ_rows - virs[y]
    wide = 2 * LANES
    into = lax.broadcasted_iota(jnp.int32, (wide, wide), 1)
    middle = jnp.where(into < LANES, into + PART, into - PART)
    source = jnp.where((into >= PART) & (into < wide - PART), middle, into)
    reorder = (lax.broadcasted_iota(jnp.int32, (wide, wide), 0) == source).astype(jnp.float32).astype(jnp.bfloat16)

    def split_columns(i, block):
        for p in range(NEED // 2):
            moved = jnp.dot(block[:, p * wide:(p + 1) * wide], reorder, preferred_element_type=jnp.float32)
            moved = moved.astype(jnp.bfloat16)
            rows_low[i, :, p * LANES:(p + 1) * LANES] = moved[:, :LANES]
            rows_high[i, :, p * LANES:(p + 1) * LANES] = moved[:, LANES:]

    split_columns(0, a0)
    arrived(a0, y_recv.at[1])
    split_columns(1, ap)
    split_columns(2, am)
    arrived(got[0].at[pl.ds(0, ARRIVING)], got_recv.at[0])
    for t in range(NEED):
        tile = got[0][own_tab[0, t]]
        stack_low[pl.ds(t * PART, PART)] = tile
    for i in range(3):
        mine[i] = jnp.dot(rows_low[i], stack_low[...], preferred_element_type=jnp.float32)
    arrived(ao, y_recv.at[2])
    split_columns(3, ao)
    mine[3] = jnp.dot(rows_low[3], stack_low[...], preferred_element_type=jnp.float32)
    arrived(got[1].at[pl.ds(0, ARRIVING)], got_recv.at[1])
    for t in range(NEED):
        tile = got[1][own_tab[0, t]]
        stack_high[pl.ds(t * PART, PART)] = tile

    square = jnp.zeros((8, LANES), jnp.float32)
    for dy, i in ((0, 0), (1, 1), (3, 2), (2, 3)):
        ladder = mine[i] + jnp.dot(rows_high[i], stack_high[...], preferred_element_type=jnp.float32)
        update = ladder / gaps[dy]
        square = square + jnp.sum((update * update).reshape(rows // 8, 8, LANES), axis=0)
        if dy == 0:
            cols[y] = update
        else:
            sent[dy] = update

    spot = z * 2 + c
    sum1[spot] = jnp.sum(square, axis=0, keepdims=True)
    for dz in (4, 3, 5, 2, 6, 1, 7, 0):
        for dc in (1, 0):
            if (dz, dc) != (0, 0):
                send(sum1.at[spot], sum1.at[spot], s_send.at[0], s_recv.at[0], at(0, 0, dz, dc))
    for dy in (1, 2, 3):
        send(sent.at[dy], cols.at[y], u_sem.at[0], u_sem.at[1], at(0, dy, 0, 0))
    left_here(a0, y_send.at[1])
    left_here(ao, y_send.at[2])
    left_here(occs.at[pl.ds(0, 3)], occ_sem.at[0])
    for hop in range(2):
        left_here(got[0].at[pl.ds(0, 4 * CD_DEV)], z_send.at[hop])
    for h in range(PARTS):
        left_here(sx[h], x_send.at[h])
        left_here(sd[h], d_send.at[h])
        left_here(got[h].at[pl.ds(0, PASSED_ON)], f_send.at[h])
    arrived(sum1.at[pl.ds(0, 15)], s_recv.at[0])
    spot = x * NY + y
    sum2[spot] = jnp.sum(sum1[...], axis=0)
    for dx in (2, 1, 3, 0):
        for dy in (2, 1, 3, 0):
            if (dx, dy) != (0, 0):
                send(sum2.at[spot], sum2.at[spot], s_send.at[1], s_recv.at[1], at(dx, dy, 0, 0))
    left_here(sum1.at[pl.ds(0, 15)], s_send.at[0])
    arrived(cols.at[pl.ds(0, 3)], u_sem.at[1])
    stores = []
    for k in range(NY):
        stores.append(pltpu.make_async_copy(cols.at[k], out.at[:, pl.ds(k * LANES, LANES)], load_sem.at[k]))
        stores[k].start()
    left_here(cols.at[pl.ds(0, 3)], u_sem.at[0])
    arrived(sum2.at[pl.ds(0, 15)], s_recv.at[1])
    everything = jnp.sum(jnp.sum(sum2[...], axis=0), axis=1, keepdims=True)
    rms[...] = jnp.sqrt(everything / total_entries)
    for copy in stores:
        copy.wait()
    left_here(sum2.at[pl.ds(0, 15)], s_send.at[1])


def per_device(amplitudes, integrals, task_owner, task_slot, occ_pair, vir_pair):
    rows, depth = amplitudes.shape
    columns = integrals.shape[1]
    bf16, f32, i32 = jnp.bfloat16, jnp.float32, jnp.int32
    dma = pltpu.SemaphoreType.DMA

    def body(*refs):
        kernel(rows, float(rows * OWNERS * NY * columns), *refs)

    def parts(*lead):
        return [pltpu.VMEM((*lead, size, LANES), bf16) for size in SIZES]

    anywhere, vmem = pl.BlockSpec(memory_space=pltpu.HBM), pl.BlockSpec(memory_space=pltpu.VMEM)
    update, rms = pl.pallas_call(
        body,
        out_shape=(
            jax.ShapeDtypeStruct((rows, columns), f32),
            jax.ShapeDtypeStruct((1, 1), f32),
        ),
        in_specs=[anywhere] * 6,
        out_specs=(anywhere, vmem),
        scratch_shapes=[
            *[pltpu.VMEM((1, OWNERS * NEED), i32)] * 2,
            *[pltpu.VMEM((OWNERS, NEED), i32)] * 2,
            pltpu.VMEM((OWNERS, LANES), i32),
            pltpu.VMEM((8, LANES), i32),
            pltpu.SMEM((OWNERS, LANES), i32),
            pltpu.SMEM((8, LANES), i32),
            *parts(CD_DEV), *parts(CD_DEV), *parts(CD_DEV), *parts(CD_DEV), *parts(CD_DEV),
            *parts(2 * OWNERS), *parts(5, 7, 2), *parts(24, 2),
            *parts(16), *parts(8), *parts(16), *parts(8),
            *[pltpu.VMEM((rows, depth), bf16)] * 4,
            *[pltpu.VMEM((depth // 2, LANES), bf16)] * 2,
            *[pltpu.VMEM((NY, rows, depth // 2), bf16)] * 2,
            *[pltpu.VMEM((NY, rows, LANES), f32)] * 4,
            pltpu.VMEM((NY, 1, rows), f32),
            pltpu.VMEM((NY, 1, LANES), f32),
            *[pltpu.VMEM((16, 1, LANES), f32)] * 2,
            dma((7,)), dma((PARTS,)),
            dma((2,)), dma((2, PARTS)),
            dma((3,)), dma((3,)),
            dma((PARTS,)), dma((PARTS,)), dma((PARTS,)), dma((PARTS, 2)), dma((PARTS,)),
            dma((2,)), dma((2,)), dma((2,)), dma((2,)),
        ],
        compiler_params=pltpu.CompilerParams(
            collective_id=0, has_side_effects=True, vmem_limit_bytes=56 << 20
        ),
        cost_estimate=pl.CostEstimate(
            flops=2 * rows * depth * columns, bytes_accessed=8 << 20, transcendentals=0
        ),
        name="ladder",
    )(
        task_owner.T,
        task_slot.T,
        integrals.reshape(CD_DEV, TILE, columns),
        amplitudes,
        occ_pair.reshape(1, rows),
        vir_pair.reshape(NY, 1, LANES),
    )
    return update, rms[0, 0]


def solution(mesh):
    placed = (P(("own", "grp"), None), P("own", None), P(), P(), P(("own", "grp")), P())
    return jax.shard_map(
        per_device,
        mesh=mesh,
        in_specs=placed,
        out_specs=(P(("own", "grp"), None), P()),
        check_vma=False,
    )
```
